32 devices in a mesh: grp: 4 (over y, x), band: 8 (over z, core).
Axes of the slice: x: 2, y: 2, z: 4, core: 2. Of those that a mesh axis runs over, the one named last changes fastest.
Arguments:
- raw: bfloat16 [2, 256, 16384], P(None, 'band', 'grp'), may hold values from -6 to 6
- taps: int32 [5, 2, 4, 512], replicated, may hold values from 0 to 255, as said below
- weights: float32 [5, 2, 4, 512], replicated, may hold values from -0.11 to 1.6, as said below
- shifts: float32 [5], replicated, may hold values from 1 to 3
Outputs:
- image: bfloat16 [2, 16384, 256], P(None, ('grp', 'band'))
The draws below stay inside these ranges and needn't reach their ends.
Inputs may be any that keep to these rules, and one draw needn't show every extreme that they name: taps[l, h, s, j] = c - 1 + s clipped to the half sector, where c is j / 2 or (j + 1) / 2 rounded down, clipped likewise. `weights`: each group of four coefficients is a cubic Lagrange stencil times a positive factor.
All inputs are finite; a program needn't handle non-finite values.
Results may differ from the reference program's by a relative error of at most 0.011.
Values may be sent and summed in bfloat16 or wider, within the bound.
No kernel may reach another device: no remote copies, remote signals or barrier semaphores. Data moves between devices by JAX's collectives and lax.ppermute only.
A program may use at most 64 MiB of HBM per device.

```python
import math
import jax
import jax.numpy as jnp
import numpy as np
from jax import lax

NF = 256
ANGLES = 512
PULSE_DEV = 512
BAND_LEVELS = 3
LEVELS = 5
PULSES = 16384
N_GRP = 4
N_BAND = 8


def draw_taps(key, part):
    half_len = ANGLES // 2
    nudge = jax.random.randint(jax.random.fold_in(key, 11), (LEVELS, 2, 1, ANGLES), 0, 2)
    centre = jnp.clip((jnp.arange(ANGLES, dtype=jnp.int32)[None, None, None, :] + nudge) // 2, 0, half_len - 1)
    offsets = jnp.arange(4, dtype=jnp.int32)[None, None, :, None] - 1
    return jnp.clip(centre + offsets, 0, half_len - 1).astype(jnp.int32)


def draw_weights(key, part):
    fraction = jax.random.uniform(jax.random.fold_in(key, 21), (LEVELS, 2, 1, ANGLES), dtype=jnp.float32)
    row_gain = jnp.exp(jax.random.uniform(jax.random.fold_in(key, 22), (LEVELS, 2, 1, ANGLES), dtype=jnp.float32, minval=math.log(0.6), maxval=math.log(1.6)))
    tap_first = -fraction * (fraction - 1.0) * (fraction - 2.0) / 6.0
    tap_second = (fraction + 1.0) * (fraction - 1.0) * (fraction - 2.0) / 2.0
    tap_third = -(fraction + 1.0) * fraction * (fraction - 2.0) / 2.0
    tap_fourth = (fraction + 1.0) * fraction * (fraction - 1.0) / 6.0
    stencil = jnp.concatenate([tap_first, tap_second, tap_third, tap_fourth], axis=2)
    return (stencil * row_gain).astype(jnp.float32)


def block_levels(stream_key, dims, pieces, least, high):
    loudness = 1.0
    for position, parts in pieces:
        draws = jax.random.uniform(jax.random.fold_in(jax.random.fold_in(stream_key, 6), position), (parts,), jnp.float32, least / len(pieces), high / len(pieces))
        loudness = loudness * jnp.repeat(jnp.exp(draws), dims[position] // parts).reshape((-1,) + (1,) * (len(dims) - 1 - position))
    return loudness


def scatter_about(key, extent, width, most, cuts=(), kind=jnp.bfloat16):
    drawn = width * jax.random.normal(key, extent, jnp.float32)
    if cuts:
        drawn = drawn * block_levels(key, extent, cuts, -0.22, 0.18)
    return jnp.clip(drawn, -most, most).astype(kind)


def setup_inputs(seed: int = 0) -> dict:
    streams_of = jax.random.split(jax.random.key(seed), 5)
    return {
        "raw": scatter_about(streams_of[0], (2, NF, PULSES), 1.0, 6.0, ((1, 8), (2, 4))),
        "taps": draw_taps(jax.random.fold_in(streams_of[4], 71), 0),
        "weights": draw_weights(jax.random.fold_in(streams_of[4], 71), 0),
        "shifts": jnp.clip(jax.random.uniform(streams_of[3], (LEVELS,), jnp.float32, 1.0, 3.0), 1.0, 3.0),
    }


inv_root_two = 0.7071067811865476

def range_table(freq_count):
    column = jnp.arange(freq_count, dtype=jnp.int32)
    phases = (column[:, None] * column[None, :] % freq_count).astype(jnp.float32) * (2.0 * math.pi / freq_count)
    cosine = jnp.cos(phases)
    sine_map = jnp.sin(phases)
    real_rows = jnp.stack([cosine, -sine_map], axis=1)
    imag_rows = jnp.stack([sine_map, cosine], axis=1)
    return jnp.stack([real_rows, imag_rows], axis=0).astype(jnp.bfloat16)

def beam_table(angles, pulses):
    angle_ids = jnp.arange(angles, dtype=jnp.int32)
    pulse_ids = jnp.arange(pulses, dtype=jnp.int32)
    phases = (angle_ids[:, None] * pulse_ids[None, :] % angles).astype(jnp.float32) * (2.0 * math.pi / angles)
    cosine = jnp.cos(phases)
    sine_map = jnp.sin(phases)
    real_rows = jnp.stack([cosine, sine_map], axis=1)
    imag_rows = jnp.stack([-sine_map, cosine], axis=1)
    return jnp.stack([real_rows, imag_rows], axis=0).astype(jnp.bfloat16)

def interp_matrix(tap_rows, weight_rows, half_len):
    onehot = tap_rows[:, :, None] == jnp.arange(half_len, dtype=jnp.int32)[None, None, :]
    matrix = lax.optimization_barrier(jnp.sum(jnp.where(onehot, weight_rows[:, :, None], jnp.zeros((), weight_rows.dtype)), axis=0))
    return matrix.astype(jnp.bfloat16)

def phase_angle(shift_now, half_bit, angles, freq_count):
    angle_pos = (half_bit * angles + jnp.arange(angles, dtype=jnp.int32)).astype(jnp.float32)
    across = (angle_pos + 0.5) / (2.0 * angles) - 0.5
    ranges = (jnp.arange(freq_count, dtype=jnp.int32) + freq_count).astype(jnp.float32) / freq_count
    return 2.0 * math.pi * shift_now * across[:, None] * ranges[None, :]

def rotate(real_part, imag_part, cosine, sine_map):
    return (cosine * real_part - sine_map * imag_part, cosine * imag_part + sine_map * real_part)

def reference(raw, taps, weights, shifts):
    tile_count = N_GRP * N_BAND
    half_len = ANGLES // 2
    samples = raw.reshape(2, NF, tile_count, PULSE_DEV)
    profile = (jnp.einsum('cftq,cfds->dtqs', samples.astype(jnp.float32), range_table(NF).astype(jnp.float32)) * (1.0 / math.sqrt(NF))).astype(jnp.bfloat16)
    images = (jnp.einsum('dacq,ctqr->tdar', beam_table(ANGLES, PULSE_DEV).astype(jnp.float32), profile.astype(jnp.float32)) * (1.0 / math.sqrt(PULSE_DEV))).astype(jnp.bfloat16)
    band_bits = N_BAND.bit_length() - 1
    numbers = np.arange(tile_count)
    for section_no in range(LEVELS):
        bit_pos = section_no if section_no < BAND_LEVELS else band_bits + section_no - BAND_LEVELS
        bit_mask = 1 << bit_pos
        merged = images
        for half_bit in (0, 1):
            chosen = numbers[numbers >> bit_pos & 1 == half_bit]
            start = half_bit * half_len
            lower_half = images[chosen & ~bit_mask][:, :, start:start + half_len]
            upper_half = images[chosen | bit_mask][:, :, start:start + half_len]
            matrix = interp_matrix(taps[section_no, half_bit], weights[section_no, half_bit], half_len).astype(jnp.float32)
            low_prod = jnp.einsum('jk,tcks->tcjs', matrix, lower_half.astype(jnp.float32))
            up_prod = jnp.einsum('jk,tcks->tcjs', matrix, upper_half.astype(jnp.float32))
            angle_map = phase_angle(shifts[section_no], half_bit, ANGLES, NF)
            cosine = jnp.cos(angle_map)
            sine_map = jnp.sin(angle_map)
            low_re, low_im = rotate(low_prod[:, 0], low_prod[:, 1], cosine, sine_map)
            up_re, up_im = rotate(up_prod[:, 0], up_prod[:, 1], cosine, -sine_map)
            merged_block = (jnp.stack([low_re + up_re, low_im + up_im], axis=1) * inv_root_two).astype(jnp.bfloat16)
            merged = merged.at[chosen].set(merged_block)
        images = merged
    return jnp.transpose(images, (1, 0, 2, 3)).reshape(2, tile_count * ANGLES, NF)
```

```python
import functools
import math

import jax
import jax.numpy as jnp
import ml_dtypes
import numpy as np
from jax import lax
from jax.experimental import pallas as pl
from jax.experimental.pallas import tpu as pltpu
from jax.sharding import PartitionSpec as P

ANGLES = 512
HALF = ANGLES // 2
BAND_LEVELS = 3
GRP_LEVELS = 2
LEVELS = BAND_LEVELS + GRP_LEVELS
SUBS = 1 << BAND_LEVELS
MATES = 1 << GRP_LEVELS
ROOT_HALF = 0.7071067811865476


def up_to(value, unit):
    return -(-value // unit) * unit


def rows_read(low, high):
    return max(0, low // 2 - 1), min(HALF - 1, (high + 1) // 2 + 2)


WIDE = up_to(rows_read(0, HALF - 1)[1] + 1, 16)
WIDE_STEP = HALF - WIDE


def first_windows():
    spans = []
    for h2 in (0, 1):
        low, high = rows_read(h2 * HALF, h2 * HALF + HALF - 1)
        for h1 in (0, 1):
            spans.append(rows_read(h1 * HALF + low, h1 * HALF + high))
    rows = up_to(max(high - low + 1 for low, high in spans), 8)
    return [min(low, HALF - rows) for low, high in spans], rows


FIRST_STARTS, FIRST = first_windows()
FIRST_PAD = up_to(FIRST, 16)


def beam_rows(pulses):
    pulse_ids = np.arange(pulses)
    sectors = []
    for sector in range(SUBS):
        start = (sector & 1) * HALF + FIRST_STARTS[sector >> 1]
        angle_ids = start + np.arange(FIRST)
        phases = (angle_ids[:, None] * pulse_ids[None, :] % ANGLES) * (2.0 * math.pi / ANGLES)
        sectors.append(np.concatenate([np.cos(phases), np.sin(phases)], axis=1))
    return np.concatenate(sectors, axis=0).astype(ml_dtypes.bfloat16)


def range_rows(freq_count, freq_local):
    ids = np.arange(freq_count)
    phases = (ids[:, None] * ids[None, :] % freq_count) * (2.0 * math.pi / freq_count)
    cosine, sine = np.cos(phases), np.sin(phases)
    table = np.stack(
        [np.concatenate([cosine, -sine], axis=1), np.concatenate([sine, cosine], axis=1)]
    )
    table = table.reshape(2, freq_count // freq_local, freq_local, 2 * freq_count)
    table = table.transpose(1, 0, 2, 3).reshape(-1, 2 * freq_local, 2 * freq_count)
    return table.astype(ml_dtypes.bfloat16)


def beam_kernel(pos, raw, table, *rest, pulses):
    outs, (rhs, acc) = rest[:-2], rest[-2:]
    freqs = raw.shape[1]
    band_pos = pos[0]
    scale = 1.0 / math.sqrt(pulses)
    for upper in range(len(outs) // SUBS):
        block = band_pos // SUBS ^ upper
        for t in range(SUBS):
            at = pl.multiple_of((block * SUBS + t) * pulses, pulses)
            real = raw[0, :, pl.ds(at, pulses)]
            imag = raw[1, :, pl.ds(at, pulses)]
            row = t * 2 * freqs
            rhs[row : row + freqs, :pulses] = real
            rhs[row : row + freqs, pulses:] = imag
            rhs[row + freqs : row + 2 * freqs, :pulses] = imag
            rhs[row + freqs : row + 2 * freqs, pulses:] = -real
        acc[...] = lax.dot_general(
            table[...], rhs[...], (((1,), (1,)), ((), ())), preferred_element_type=jnp.float32
        )
        for low in range(SUBS):
            sector = (band_pos ^ low) & (SUBS - 1)
            start = pl.multiple_of(sector * FIRST, 8)
            outs[upper * SUBS + low][...] = (acc[pl.ds(start, FIRST), :] * scale).astype(
                jnp.bfloat16
            )


def interp_t(taps, weights, start, rows):
    row_ids = lax.broadcasted_iota(jnp.int32, (rows, ANGLES), 0) + start
    total = jnp.zeros((rows, ANGLES), jnp.float32)
    for s in range(taps.shape[0]):
        total += jnp.where(row_ids == taps[s : s + 1, :], weights[s : s + 1, :], 0.0)
    return total


def phase_rows(cos_ref, sin_ref, shift, first, count, sign):
    freqs = cos_ref.shape[1]
    ranges = (
        (lax.broadcasted_iota(jnp.int32, (1, freqs), 1) + freqs).astype(jnp.float32)
        * (2.0 * math.pi / freqs)
        * shift
    )
    groups = count // 8
    coarse_ids = lax.broadcasted_iota(jnp.int32, (groups, 1), 0) * 8 + first
    coarse = ((coarse_ids.astype(jnp.float32) + 0.5) / (2.0 * ANGLES) - 0.5) * ranges
    fine_ids = lax.broadcasted_iota(jnp.int32, (8, 1), 0)
    fine = (fine_ids.astype(jnp.float32) / (2.0 * ANGLES)) * ranges
    coarse_cos, coarse_sin = jnp.cos(coarse) * ROOT_HALF, jnp.sin(coarse) * ROOT_HALF
    fine_cos, fine_sin = jnp.cos(fine), jnp.sin(fine)
    for group in range(groups):
        c, s = coarse_cos[group : group + 1], coarse_sin[group : group + 1]
        cos_ref[group * 8 : group * 8 + 8, :] = c * fine_cos - s * fine_sin
        sin_ref[group * 8 : group * 8 + 8, :] = sign * (s * fine_cos + c * fine_sin)


def table_kernel(
    pos, shifts, taps, weights, ranges,
    range_out, m0, m1, m2, m3, m4, c0, s0, c1, s1, c2, s2, c3, s3, c4, s4, turned,
):
    band_pos, grp_pos = pos[0], pos[1]
    h0, h1, h2 = band_pos & 1, band_pos >> 1 & 1, band_pos >> 2 & 1
    h3, h4 = grp_pos & 1, grp_pos >> 1 & 1
    count = ranges.shape[0]
    depth = ranges.shape[1]
    for k in range(count):
        range_out[k * depth : (k + 1) * depth, :] = ranges[band_pos ^ k]

    def fill(out, level, half, start, rows, first, count, row=0):
        turned[:, :rows] = interp_t(taps[level, half], weights[level, half], start, rows).T
        out[row : row + count, :rows] = turned[pl.ds(first, count), :rows].astype(jnp.bfloat16)

    first_start = FIRST_STARTS[0]
    for combo in range(1, len(FIRST_STARTS)):
        first_start = jnp.where(h1 + 2 * h2 == combo, FIRST_STARTS[combo], first_start)
    wide1 = pl.multiple_of(h1 * HALF + h2 * WIDE_STEP, 16)
    sum_rows = interp_t(taps[0, h0], weights[0, h0], first_start, FIRST_PAD)
    turned[:, :FIRST_PAD] = sum_rows.T
    window = turned[pl.ds(wide1, WIDE), :FIRST_PAD].astype(jnp.bfloat16)
    m0[:WIDE, :FIRST_PAD] = window
    m0[:WIDE, FIRST_PAD:] = window
    m0[WIDE:, :FIRST_PAD] = window
    m0[WIDE:, FIRST_PAD:] = -window
    phase_rows(c0, s0, shifts[0], h0 * ANGLES + wide1, WIDE, 1.0)

    half2 = pl.multiple_of(h2 * HALF, HALF)
    fill(m1, 1, h1, h2 * WIDE_STEP, WIDE, half2, HALF)
    phase_rows(c1, s1, shifts[1], h1 * ANGLES + half2, HALF, 1.0)

    turned[...] = interp_t(taps[2, h2], weights[2, h2], 0, HALF).T
    for k in range(MATES):
        mate = grp_pos ^ k
        at = pl.multiple_of((mate & 1) * HALF + (mate >> 1 & 1) * WIDE_STEP, 16)
        m2[k * WIDE : (k + 1) * WIDE, :] = turned[pl.ds(at, WIDE), :].astype(jnp.bfloat16)
        rows = pl.ds(k * WIDE, WIDE)
        phase_rows(c2.at[rows], s2.at[rows], shifts[2], h2 * ANGLES + at, WIDE, 1.0)

    half4 = pl.multiple_of(h4 * HALF, HALF)
    fill(m3, 3, h3, h4 * WIDE_STEP, WIDE, half4, HALF)
    sign3 = (1 - 2 * h3).astype(jnp.float32)
    phase_rows(c3, s3, shifts[3], h3 * ANGLES + half4, HALF, sign3)
    fill(m4, 4, h4, 0, HALF, 0, ANGLES)
    sign4 = (1 - 2 * h4).astype(jnp.float32)
    phase_rows(c4, s4, shifts[4], h4 * ANGLES, ANGLES, sign4)


def dot(left, right):
    return jnp.dot(left, right, preferred_element_type=jnp.float32)


def turn(out, rows, total, diff, cosine, sine):
    freqs = cosine.shape[1]
    out[rows, :freqs] = (cosine * total[:, :freqs] - sine * diff[:, freqs:]).astype(out.dtype)
    out[rows, freqs:] = (cosine * total[:, freqs:] + sine * diff[:, :freqs]).astype(out.dtype)


def band_kernel(*refs, sources):
    blocks = refs[:sources]
    ranges, m0, m1, m2, c0, s0, c1, s1, c2, s2 = refs[sources : sources + 10]
    outs = refs[sources + 10 : sources + 10 + MATES]
    wide, sub0, sub1, sub2 = refs[sources + 10 + MATES :]
    depth = blocks[0].shape[1] // SUBS
    freqs = c0.shape[1]
    scale = 1.0 / math.sqrt(freqs)
    for t in range(SUBS):
        row = t * FIRST_PAD
        if FIRST_PAD > FIRST:
            wide[row + FIRST : row + FIRST_PAD, :] = jnp.zeros(
                (FIRST_PAD - FIRST, wide.shape[1]), wide.dtype
            )
        for k in range(sources):
            wide[row : row + FIRST, k * depth : (k + 1) * depth] = blocks[k][
                :, t * depth : (t + 1) * depth
            ]
    sub0[...] = (dot(wide[...], ranges[...]) * scale).astype(sub0.dtype)
    for p in range(SUBS // 2):
        both = dot(m0[...], sub0[2 * p * FIRST_PAD : 2 * (p + 1) * FIRST_PAD, :])
        turn(sub1, slice(p * WIDE, (p + 1) * WIDE), both[:WIDE], both[WIDE:], c0[...], s0[...])
    for p in range(SUBS // 4):
        low = dot(m1[...], sub1[2 * p * WIDE : (2 * p + 1) * WIDE, :])
        high = dot(m1[...], sub1[(2 * p + 1) * WIDE : (2 * p + 2) * WIDE, :])
        rows = slice(p * HALF, (p + 1) * HALF)
        turn(sub2, rows, low + high, low - high, c1[...], s1[...])
    for k in range(MATES):
        rows = slice(k * WIDE, (k + 1) * WIDE)
        low = dot(m2[rows, :], sub2[:HALF, :])
        high = dot(m2[rows, :], sub2[HALF:, :])
        turn(outs[k], slice(None), low + high, low - high, c2[rows, :], s2[rows, :])


def grp_kernel(own, along, across, both, m3, m4, c3, s3, c4, s4, out, sub4):
    freqs = c3.shape[1]
    for q, (mine, other) in enumerate(((own, along), (across, both))):
        low = dot(m3[...], mine[...])
        high = dot(m3[...], other[...])
        turn(sub4, slice(q * HALF, (q + 1) * HALF), low + high, low - high, c3[...], s3[...])
    low = dot(m4[...], sub4[:HALF, :])
    high = dot(m4[...], sub4[HALF:, :])
    total, diff = low + high, low - high
    cosine, sine = c4[...], s4[...]
    out[0] = (cosine * total[:, :freqs] - sine * diff[:, freqs:]).astype(out.dtype)
    out[1] = (cosine * total[:, freqs:] + sine * diff[:, :freqs]).astype(out.dtype)


VMEM = pl.BlockSpec(memory_space=pltpu.VMEM)
SMEM = pl.BlockSpec(memory_space=pltpu.SMEM)
PARAMS = pltpu.CompilerParams(vmem_limit_bytes=48 * 1024 * 1024)


def swapped(block, axis, mask):
    count = lax.axis_size(axis)
    return lax.ppermute(block, axis, [(low, low ^ mask) for low in range(count)])


def on_device(raw, taps, weights, shifts):
    n_band = lax.axis_size("band")
    freqs = raw.shape[1]
    freq_count = freqs * n_band
    pulses = raw.shape[2] // n_band
    bf16, f32 = jnp.bfloat16, jnp.float32
    shape = jax.ShapeDtypeStruct
    pos = jnp.stack([lax.axis_index("band"), lax.axis_index("grp")]).astype(jnp.int32)
    lanes = SUBS * 2 * freqs

    beams = pl.pallas_call(
        functools.partial(beam_kernel, pulses=pulses),
        out_shape=[shape((FIRST, lanes), bf16)] * n_band,
        in_specs=[SMEM, VMEM, VMEM],
        out_specs=[VMEM] * n_band,
        scratch_shapes=[
            pltpu.VMEM((lanes, 2 * pulses), bf16),
            pltpu.VMEM((SUBS * FIRST, lanes), f32),
        ],
        compiler_params=PARAMS,
        cost_estimate=pl.CostEstimate(
            flops=2 * SUBS * FIRST * 2 * pulses * lanes, bytes_accessed=1 << 21, transcendentals=0
        ),
        name="beam",
    )(pos, raw, jnp.asarray(beam_rows(pulses)))

    wide2 = 2 * freq_count
    tables = pl.pallas_call(
        table_kernel,
        out_shape=[
            shape((wide2, wide2), bf16),
            shape((2 * WIDE, 2 * FIRST_PAD), bf16),
            shape((HALF, WIDE), bf16),
            shape((MATES * WIDE, HALF), bf16),
            shape((HALF, WIDE), bf16),
            shape((ANGLES, HALF), bf16),
        ]
        + [
            shape((rows, freq_count), f32)
            for rows in (WIDE, HALF, MATES * WIDE, HALF, ANGLES)
            for _ in range(2)
        ],
        in_specs=[SMEM, SMEM, VMEM, VMEM, VMEM],
        out_specs=[VMEM] * 16,
        scratch_shapes=[pltpu.VMEM((ANGLES, HALF), f32)],
        compiler_params=PARAMS,
        cost_estimate=pl.CostEstimate(
            flops=1 << 24, bytes_accessed=1 << 23, transcendentals=1 << 18
        ),
        name="tables",
    )(pos, shifts, taps, weights, jnp.asarray(range_rows(freq_count, freqs)))
    ranges, m0, m1, m2, m3, m4, c0, s0, c1, s1, c2, s2, c3, s3, c4, s4 = tables

    blocks = [beams[0]] + [swapped(beams[k], "band", k) for k in range(1, n_band)]
    pieces = pl.pallas_call(
        functools.partial(band_kernel, sources=n_band),
        out_shape=[shape((WIDE, wide2), bf16)] * MATES,
        in_specs=[VMEM] * (n_band + 10),
        out_specs=[VMEM] * MATES,
        scratch_shapes=[
            pltpu.VMEM((SUBS * FIRST_PAD, wide2), bf16),
            pltpu.VMEM((SUBS * FIRST_PAD, wide2), bf16),
            pltpu.VMEM((SUBS // 2 * WIDE, wide2), bf16),
            pltpu.VMEM((SUBS // 4 * HALF, wide2), bf16),
        ],
        compiler_params=PARAMS,
        cost_estimate=pl.CostEstimate(flops=1 << 31, bytes_accessed=1 << 22, transcendentals=0),
        name="band_merges",
    )(*blocks, ranges, m0, m1, m2, c0, s0, c1, s1, c2, s2)

    halves = [pieces[0]] + [swapped(pieces[k], "grp", k) for k in range(1, MATES)]
    return pl.pallas_call(
        grp_kernel,
        out_shape=shape((2, ANGLES, freq_count), bf16),
        in_specs=[VMEM] * 10,
        out_specs=VMEM,
        scratch_shapes=[pltpu.VMEM((2 * HALF, wide2), bf16)],
        compiler_params=PARAMS,
        cost_estimate=pl.CostEstimate(flops=1 << 30, bytes_accessed=1 << 22, transcendentals=0),
        name="grp_merges",
    )(*halves, m3, m4, c3, s3, c4, s4)


def solution(mesh):
    in_specs = (P(None, "band", "grp"), P(), P(), P())
    out_specs = P(None, ("grp", "band"), None)
    return jax.shard_map(
        on_device, mesh=mesh, in_specs=in_specs, out_specs=out_specs, check_vma=False
    )
```

```python
import functools
import math

import jax
import jax.numpy as jnp
import ml_dtypes
import numpy as np
from jax import lax
from jax.experimental import pallas as pl
from jax.experimental.pallas import tpu as pltpu
from jax.sharding import PartitionSpec as P

ANGLES = 512
HALF = ANGLES // 2
BAND_LEVELS = 3
GRP_LEVELS = 2
LEVELS = BAND_LEVELS + GRP_LEVELS
SUBS = 1 << BAND_LEVELS
MATES = 1 << GRP_LEVELS
ROOT_HALF = 0.7071067811865476


def up_to(value, unit):
    return -(-value // unit) * unit


def rows_read(low, high):
    return max(0, low // 2 - 1), min(HALF - 1, (high + 1) // 2 + 2)


WIDE = up_to(rows_read(0, HALF - 1)[1] + 1, 16)
WIDE_STEP = HALF - WIDE
SENT = up_to(rows_read(0, HALF - 1)[1] + 1, 8)
SENT_STEP = HALF - SENT


def first_windows():
    spans = []
    for h2 in (0, 1):
        low, high = rows_read(h2 * HALF, h2 * HALF + HALF - 1)
        for h1 in (0, 1):
            spans.append(rows_read(h1 * HALF + low, h1 * HALF + high))
    rows = up_to(max(high - low + 1 + low % 2 for low, high in spans), 8)
    return [min(low - low % 2, HALF - rows) for low, high in spans], rows


FIRST_STARTS, FIRST = first_windows()
FIRST_PAD = up_to(FIRST, 16)
FIRST_SIDE = up_to(FIRST // 2, 8)


def beam_rows(pulses):
    pulse_ids = np.arange(pulses // 2)
    sides = []
    for odd in (0, 1):
        sectors = np.zeros((SUBS, FIRST_SIDE, pulses))
        for sector in range(SUBS):
            start = (sector & 1) * HALF + FIRST_STARTS[sector >> 1]
            angle_ids = start + 2 * np.arange(FIRST // 2) + odd
            phases = (angle_ids[:, None] * pulse_ids[None, :] % ANGLES) * (2.0 * math.pi / ANGLES)
            sectors[sector, : FIRST // 2] = np.concatenate([np.cos(phases), np.sin(phases)], axis=1)
        sides.append(sectors.reshape(SUBS * FIRST_SIDE, pulses))
    return np.stack(sides).astype(ml_dtypes.bfloat16)


def range_rows(freq_count, freq_local):
    ids = np.arange(freq_count)
    phases = (ids[:, None] * ids[None, :] % freq_count) * (2.0 * math.pi / freq_count)
    cosine, sine = np.cos(phases), np.sin(phases)
    table = np.stack(
        [np.concatenate([cosine, -sine], axis=1), np.concatenate([sine, cosine], axis=1)]
    )
    table = table.reshape(2, freq_count // freq_local, freq_local, 2 * freq_count)
    table = table.transpose(1, 0, 2, 3).reshape(-1, 2 * freq_local, 2 * freq_count)
    return table.astype(ml_dtypes.bfloat16)


def beam_kernel(raw_far, table_far, *refs, pulses):
    outs, (raw, table, rhs, acc, raw_sem, table_sem) = refs[:-6], refs[-6:]
    freqs = raw.shape[1]
    half = pulses // 2
    band_pos = lax.axis_index("band")
    scale = 1.0 / math.sqrt(pulses)
    raw_copy = pltpu.make_async_copy(raw_far, raw, raw_sem)
    raw_copy.start()
    table_copy = pltpu.make_async_copy(table_far, table, table_sem)
    table_copy.start()
    raw_copy.wait()
    for upper in range(len(outs) // SUBS):
        block = band_pos // SUBS ^ upper if len(outs) > SUBS else 0
        for t in range(SUBS):
            at = pl.multiple_of((block * SUBS + t) * pulses, pulses)
            row = t * 2 * freqs
            first = raw[:, :, pl.ds(at, half)]
            second = raw[:, :, pl.ds(at + half, half)]
            for side, mixed in enumerate((first + second, first - second)):
                rhs[side, row : row + freqs, :half] = mixed[0]
                rhs[side, row : row + freqs, half:] = mixed[1]
                rhs[side, row + freqs : row + 2 * freqs, :half] = mixed[1]
                rhs[side, row + freqs : row + 2 * freqs, half:] = -mixed[0]
        if upper == 0:
            table_copy.wait()
        for side in (0, 1):
            acc[side] = lax.dot_general(
                table[side],
                rhs[side],
                (((1,), (1,)), ((), ())),
                preferred_element_type=jnp.float32,
            )
        for low in range(SUBS):
            sector = (band_pos ^ low) & (SUBS - 1)
            rows = pl.ds(pl.multiple_of(sector * FIRST_SIDE, 8), FIRST // 2)
            both = jnp.concatenate([acc[0, rows, :], acc[1, rows, :]], axis=0)
            outs[upper * SUBS + low][...] = (both * scale).astype(jnp.bfloat16)


def interp_t(taps, weights, start, rows, mixed=False):
    row_ids = lax.broadcasted_iota(jnp.int32, (rows, ANGLES), 0)
    if mixed:
        side = FIRST // 2
        row_ids = jnp.where(row_ids < side, 2 * row_ids, 2 * (row_ids - side) + 1)
    row_ids += start
    total = jnp.zeros((rows, ANGLES), jnp.float32)
    for s in range(taps.shape[0]):
        total += jnp.where(row_ids == taps[s : s + 1, :], weights[s : s + 1, :], 0.0)
    return total


def phase_rows(cos_ref, sin_ref, shift, first, count, sign):
    freqs = cos_ref.shape[1]
    ranges = (
        (lax.broadcasted_iota(jnp.int32, (1, freqs), 1) + freqs).astype(jnp.float32)
        * (2.0 * math.pi / freqs)
        * shift
    )
    groups = count // 8
    coarse_ids = lax.broadcasted_iota(jnp.int32, (groups, 1), 0) * 8 + first
    coarse = ((coarse_ids.astype(jnp.float32) + 0.5) / (2.0 * ANGLES) - 0.5) * ranges
    fine_ids = lax.broadcasted_iota(jnp.int32, (8, 1), 0)
    fine = (fine_ids.astype(jnp.float32) / (2.0 * ANGLES)) * ranges
    coarse_cos, coarse_sin = jnp.cos(coarse) * ROOT_HALF, jnp.sin(coarse) * ROOT_HALF
    fine_cos, fine_sin = jnp.cos(fine), jnp.sin(fine)
    for group in range(groups):
        c, s = coarse_cos[group : group + 1], coarse_sin[group : group + 1]
        cos_ref[group * 8 : group * 8 + 8, :] = c * fine_cos - s * fine_sin
        sin_ref[group * 8 : group * 8 + 8, :] = sign * (s * fine_cos + c * fine_sin)


def table_kernel(
    shifts, taps, weights, ranges,
    range_out, m0, m1, m2, m3, m4, c0, s0, c1, s1, c2, s2, c3, s3, c4, s4, turned,
):
    band_pos, grp_pos = lax.axis_index("band"), lax.axis_index("grp")
    h0, h1, h2 = band_pos & 1, band_pos >> 1 & 1, band_pos >> 2 & 1
    h3, h4 = grp_pos & 1, grp_pos >> 1 & 1
    count = ranges.shape[0]
    depth = ranges.shape[1]
    for k in range(count):
        range_out[k * depth : (k + 1) * depth, :] = ranges[band_pos ^ k]

    def fill(out, level, half, start, rows, first, count, row=0):
        turned[:, :rows] = interp_t(taps[level, half], weights[level, half], start, rows).T
        out[row : row + count, :rows] = turned[pl.ds(first, count), :rows].astype(jnp.bfloat16)

    first_start = FIRST_STARTS[0]
    for combo in range(1, len(FIRST_STARTS)):
        first_start = jnp.where(h1 + 2 * h2 == combo, FIRST_STARTS[combo], first_start)
    wide1 = pl.multiple_of(h1 * HALF + h2 * WIDE_STEP, 16)
    sum_rows = interp_t(taps[0, h0], weights[0, h0], first_start, FIRST_PAD, True)
    turned[:, :FIRST_PAD] = sum_rows.T
    window = turned[pl.ds(wide1, WIDE), :FIRST_PAD].astype(jnp.bfloat16)
    m0[:WIDE, :FIRST_PAD] = window
    m0[:WIDE, FIRST_PAD:] = window
    m0[WIDE:, :FIRST_PAD] = window
    m0[WIDE:, FIRST_PAD:] = -window
    phase_rows(c0, s0, shifts[0], h0 * ANGLES + wide1, WIDE, 1.0)

    half2 = pl.multiple_of(h2 * HALF, HALF)
    fill(m1, 1, h1, h2 * WIDE_STEP, WIDE, half2, HALF)
    phase_rows(c1, s1, shifts[1], h1 * ANGLES + half2, HALF, 1.0)

    turned[...] = interp_t(taps[2, h2], weights[2, h2], 0, HALF).T
    for k in range(MATES):
        mate = grp_pos ^ k
        at = pl.multiple_of((mate & 1) * HALF + (mate >> 1 & 1) * SENT_STEP, 8)
        m2[k] = turned[pl.ds(at, SENT), :].astype(jnp.bfloat16)
        phase_rows(c2.at[k], s2.at[k], shifts[2], h2 * ANGLES + at, SENT, 1.0)

    half4 = pl.multiple_of(h4 * HALF, HALF)
    fill(m3, 3, h3, h4 * SENT_STEP, SENT, half4, HALF)
    sign3 = (1 - 2 * h3).astype(jnp.float32)
    phase_rows(c3, s3, shifts[3], h3 * ANGLES + half4, HALF, sign3)
    fill(m4, 4, h4, 0, HALF, 0, ANGLES)
    sign4 = (1 - 2 * h4).astype(jnp.float32)
    phase_rows(c4, s4, shifts[4], h4 * ANGLES, ANGLES, sign4)


def send_order(count):
    return [7, 6, 5, 3, 4, 2, 1, 0] if count == SUBS else list(range(count - 1, -1, -1))


def dot(left, right):
    return jnp.dot(left, right, preferred_element_type=jnp.float32)


def turn(out, rows, total, diff, cosine, sine):
    freqs = cosine.shape[1]
    out[rows, :freqs] = (cosine * total[:, :freqs] - sine * diff[:, freqs:]).astype(out.dtype)
    out[rows, freqs:] = (cosine * total[:, freqs:] + sine * diff[:, :freqs]).astype(out.dtype)


def band_kernel(*refs, sources):
    order = send_order(sources)
    blocks = [refs[order.index(k)] for k in range(sources)]
    ranges, m0, m1, m2, c0, s0, c1, s1, c2, s2 = refs[sources : sources + 10]
    outs = refs[sources + 10 : sources + 10 + MATES]
    wide, sub0, sub1, sub2 = refs[sources + 10 + MATES :]
    depth = blocks[0].shape[1] // SUBS
    freqs = c0.shape[1]
    scale = 1.0 / math.sqrt(freqs)
    for t in range(SUBS):
        row = t * FIRST_PAD
        if FIRST_PAD > FIRST:
            wide[row + FIRST : row + FIRST_PAD, :] = jnp.zeros(
                (FIRST_PAD - FIRST, wide.shape[1]), wide.dtype
            )
        for k in range(sources):
            wide[row : row + FIRST, k * depth : (k + 1) * depth] = blocks[k][
                :, t * depth : (t + 1) * depth
            ]
    sub0[...] = (dot(wide[...], ranges[...]) * scale).astype(sub0.dtype)
    for p in range(SUBS // 2):
        both = dot(m0[...], sub0[2 * p * FIRST_PAD : 2 * (p + 1) * FIRST_PAD, :])
        turn(sub1, slice(p * WIDE, (p + 1) * WIDE), both[:WIDE], both[WIDE:], c0[...], s0[...])
    for p in range(SUBS // 4):
        low = dot(m1[...], sub1[2 * p * WIDE : (2 * p + 1) * WIDE, :])
        high = dot(m1[...], sub1[(2 * p + 1) * WIDE : (2 * p + 2) * WIDE, :])
        rows = slice(p * HALF, (p + 1) * HALF)
        turn(sub2, rows, low + high, low - high, c1[...], s1[...])
    for k in range(MATES):
        low = dot(m2[k], sub2[:HALF, :])
        high = dot(m2[k], sub2[HALF:, :])
        turn(outs[k], slice(None), low + high, low - high, c2[k], s2[k])


def own_kernel(along, own, m3, m4, c3, s3, part, sub4):
    low = dot(m3[...], own[...])
    high = dot(m3[...], along[...])
    turn(sub4, slice(None), low + high, low - high, c3[...], s3[...])
    part[...] = dot(m4[...], sub4[...])


def grp_kernel(across, both, part, m3, m4, c3, s3, c4, s4, out_far, sub4, out, sems):
    freqs = c3.shape[1]
    low = dot(m3[...], across[...])
    high = dot(m3[...], both[...])
    turn(sub4, slice(None), low + high, low - high, c3[...], s3[...])
    pieces = sems.shape[0]
    count = out.shape[1] // pieces
    copies = []
    for piece in range(pieces):
        rows = slice(piece * count, (piece + 1) * count)
        low = part[rows, :]
        high = dot(m4[rows, :], sub4[...])
        total, diff = low + high, low - high
        cosine, sine = c4[rows, :], s4[rows, :]
        out[0, rows, :] = (cosine * total[:, :freqs] - sine * diff[:, freqs:]).astype(out.dtype)
        out[1, rows, :] = (cosine * total[:, freqs:] + sine * diff[:, :freqs]).astype(out.dtype)
        copy = pltpu.make_async_copy(
            out.at[:, rows, :], out_far.at[:, rows, :], sems.at[piece]
        )
        copy.start()
        copies.append(copy)
    for copy in copies:
        copy.wait()


VMEM = pl.BlockSpec(memory_space=pltpu.VMEM)
FAR = pl.BlockSpec(memory_space=pltpu.HBM)
SMEM = pl.BlockSpec(memory_space=pltpu.SMEM)
PARAMS = pltpu.CompilerParams(vmem_limit_bytes=48 * 1024 * 1024)
BEAM_PARAMS = pltpu.CompilerParams(vmem_limit_bytes=55687168)


def swapped(block, axis, mask):
    count = lax.axis_size(axis)
    return lax.ppermute(block, axis, [(low, low ^ mask) for low in range(count)])


def on_device(raw, taps, weights, shifts):
    n_band = lax.axis_size("band")
    freqs = raw.shape[1]
    freq_count = freqs * n_band
    pulses = raw.shape[2] // n_band
    bf16, f32 = jnp.bfloat16, jnp.float32
    shape = jax.ShapeDtypeStruct
    lanes = SUBS * 2 * freqs

    table = jnp.asarray(beam_rows(pulses))
    beams = pl.pallas_call(
        functools.partial(beam_kernel, pulses=pulses),
        out_shape=[shape((FIRST, lanes), bf16)] * n_band,
        in_specs=[FAR, FAR],
        out_specs=[VMEM] * n_band,
        scratch_shapes=[
            pltpu.VMEM(raw.shape, bf16),
            pltpu.VMEM(table.shape, bf16),
            pltpu.VMEM((2, lanes, pulses), bf16),
            pltpu.VMEM((2, SUBS * FIRST_SIDE, lanes), f32),
            pltpu.SemaphoreType.DMA,
            pltpu.SemaphoreType.DMA,
        ],
        compiler_params=BEAM_PARAMS,
        cost_estimate=pl.CostEstimate(
            flops=2 * SUBS * FIRST * pulses * lanes, bytes_accessed=1 << 21, transcendentals=0
        ),
        name="beam",
    )(raw, table)

    wide2 = 2 * freq_count
    tables = pl.pallas_call(
        table_kernel,
        out_shape=[
            shape((wide2, wide2), bf16),
            shape((2 * WIDE, 2 * FIRST_PAD), bf16),
            shape((HALF, WIDE), bf16),
            shape((MATES, SENT, HALF), bf16),
            shape((HALF, SENT), bf16),
            shape((ANGLES, HALF), bf16),
        ]
        + [
            shape(rows + (freq_count,), f32)
            for rows in ((WIDE,), (HALF,), (MATES, SENT), (HALF,), (ANGLES,))
            for _ in range(2)
        ],
        in_specs=[SMEM, VMEM, VMEM, VMEM],
        out_specs=[VMEM] * 16,
        scratch_shapes=[pltpu.VMEM((ANGLES, HALF), f32)],
        compiler_params=PARAMS,
        cost_estimate=pl.CostEstimate(
            flops=1 << 24, bytes_accessed=1 << 23, transcendentals=1 << 18
        ),
        name="tables",
    )(shifts, taps, weights, jnp.asarray(range_rows(freq_count, freqs)))
    ranges, m0, m1, m2, m3, m4, c0, s0, c1, s1, c2, s2, c3, s3, c4, s4 = tables

    blocks = [swapped(beams[k], "band", k) if k else beams[k] for k in send_order(n_band)]
    pieces = pl.pallas_call(
        functools.partial(band_kernel, sources=n_band),
        out_shape=[shape((SENT, wide2), bf16)] * MATES,
        in_specs=[VMEM] * (n_band + 10),
        out_specs=[VMEM] * MATES,
        scratch_shapes=[
            pltpu.VMEM((SUBS * FIRST_PAD, wide2), bf16),
            pltpu.VMEM((SUBS * FIRST_PAD, wide2), bf16),
            pltpu.VMEM((SUBS // 2 * WIDE, wide2), bf16),
            pltpu.VMEM((SUBS // 4 * HALF, wide2), bf16),
        ],
        compiler_params=PARAMS,
        cost_estimate=pl.CostEstimate(flops=1 << 31, bytes_accessed=1 << 22, transcendentals=0),
        name="band_merges",
    )(*blocks, ranges, m0, m1, m2, c0, s0, c1, s1, c2, s2)

    halves = [swapped(pieces[k], "grp", k) for k in range(1, MATES)] + [pieces[0]]
    along, across, both, own = halves
    part = pl.pallas_call(
        own_kernel,
        out_shape=shape((ANGLES, wide2), f32),
        in_specs=[VMEM] * 6,
        out_specs=VMEM,
        scratch_shapes=[pltpu.VMEM((HALF, wide2), bf16)],
        compiler_params=PARAMS,
        cost_estimate=pl.CostEstimate(flops=1 << 29, bytes_accessed=1 << 21, transcendentals=0),
        name="own_merge",
    )(along, own, m3, m4, c3, s3)
    return pl.pallas_call(
        grp_kernel,
        out_shape=shape((2, ANGLES, freq_count), bf16),
        in_specs=[VMEM] * 9,
        out_specs=FAR,
        scratch_shapes=[
            pltpu.VMEM((HALF, wide2), bf16),
            pltpu.VMEM((2, ANGLES, freq_count), bf16),
            pltpu.SemaphoreType.DMA((4,)),
        ],
        compiler_params=PARAMS,
        cost_estimate=pl.CostEstimate(flops=1 << 29, bytes_accessed=1 << 21, transcendentals=0),
        name="grp_merges",
    )(across, both, part, m3, m4, c3, s3, c4, s4)


def solution(mesh):
    in_specs = (P(None, "band", "grp"), P(), P(), P())
    out_specs = P(None, ("grp", "band"), None)
    return jax.shard_map(
        on_device, mesh=mesh, in_specs=in_specs, out_specs=out_specs, check_vma=False
    )
```

```python
import functools
import math

import jax
import jax.numpy as jnp
import ml_dtypes
import numpy as np
from jax import lax
from jax.experimental import pallas as pl
from jax.experimental.pallas import tpu as pltpu
from jax.sharding import PartitionSpec as P

ANGLES = 512
HALF = ANGLES // 2
BAND_LEVELS = 3
GRP_LEVELS = 2
LEVELS = BAND_LEVELS + GRP_LEVELS
SUBS = 1 << BAND_LEVELS
MATES = 1 << GRP_LEVELS
ROOT_HALF = 0.7071067811865476


def up_to(value, unit):
    return -(-value // unit) * unit


def rows_read(low, high):
    return max(0, low // 2 - 1), min(HALF - 1, (high + 1) // 2 + 2)


WIDE = up_to(rows_read(0, HALF - 1)[1] + 1, 16)
WIDE_STEP = HALF - WIDE
SENT = up_to(rows_read(0, HALF - 1)[1] + 1, 8)
SENT_STEP = HALF - SENT


def first_windows():
    spans = []
    for h2 in (0, 1):
        low, high = rows_read(h2 * HALF, h2 * HALF + HALF - 1)
        for h1 in (0, 1):
            spans.append(rows_read(h1 * HALF + low, h1 * HALF + high))
    rows = up_to(max(high - low + 1 + low % 2 for low, high in spans), 2)
    return [min(low - low % 2, HALF - rows) for low, high in spans], rows


FIRST_STARTS, FIRST = first_windows()
FIRST_SIDE = up_to(FIRST // 2, 8)
MAIN_SIDE = FIRST // 32 * 16
MAIN = 2 * MAIN_SIDE
TAIL_SIDE = FIRST // 2 - MAIN_SIDE
TAIL = 2 * TAIL_SIDE
TAIL_PAD = up_to(TAIL, 8)


def beam_rows(pulses):
    pulse_ids = np.arange(pulses // 2)
    sides = []
    for odd in (0, 1):
        sectors = np.zeros((SUBS, FIRST_SIDE, pulses))
        for sector in range(SUBS):
            start = (sector & 1) * HALF + FIRST_STARTS[sector >> 1]
            angle_ids = start + 2 * np.arange(FIRST // 2) + odd
            phases = (angle_ids[:, None] * pulse_ids[None, :] % ANGLES) * (2.0 * math.pi / ANGLES)
            sectors[sector, : FIRST // 2] = np.concatenate([np.cos(phases), np.sin(phases)], axis=1)
        sides.append(sectors.reshape(SUBS * FIRST_SIDE, pulses))
    return np.stack(sides).astype(ml_dtypes.bfloat16)


def range_rows(freq_count, freq_local):
    ids = np.arange(freq_count)
    phases = (ids[:, None] * ids[None, :] % freq_count) * (2.0 * math.pi / freq_count)
    cosine, sine = np.cos(phases), np.sin(phases)
    table = np.stack(
        [np.concatenate([cosine, -sine], axis=1), np.concatenate([sine, cosine], axis=1)]
    )
    table = table.reshape(2, freq_count // freq_local, freq_local, 2 * freq_count)
    table = table.transpose(1, 0, 2, 3).reshape(-1, 2 * freq_local, 2 * freq_count)
    return table.astype(ml_dtypes.bfloat16)


def beam_kernel(raw_far, table_far, *refs, pulses):
    outs, (raw, table, rhs, acc, raw_sem, table_sem) = refs[:-6], refs[-6:]
    freqs = raw.shape[1]
    half = pulses // 2
    band_pos = lax.axis_index("band")
    scale = 1.0 / math.sqrt(pulses)
    raw_copy = pltpu.make_async_copy(raw_far, raw, raw_sem)
    raw_copy.start()
    table_copy = pltpu.make_async_copy(table_far, table, table_sem)
    table_copy.start()
    raw_copy.wait()
    for upper in range(len(outs) // SUBS):
        block = band_pos // SUBS ^ upper if len(outs) > SUBS else 0
        for t in range(SUBS):
            at = pl.multiple_of((block * SUBS + t) * pulses, pulses)
            row = t * 2 * freqs
            first = raw[:, :, pl.ds(at, half)]
            second = raw[:, :, pl.ds(at + half, half)]
            for side, mixed in enumerate((first + second, first - second)):
                rhs[side, row : row + freqs, :half] = mixed[0]
                rhs[side, row : row + freqs, half:] = mixed[1]
                rhs[side, row + freqs : row + 2 * freqs, :half] = mixed[1]
                rhs[side, row + freqs : row + 2 * freqs, half:] = -mixed[0]
        if upper == 0:
            table_copy.wait()
        for side in (0, 1):
            acc[side] = lax.dot_general(
                table[side],
                rhs[side],
                (((1,), (1,)), ((), ())),
                preferred_element_type=jnp.float32,
            )
        for low in range(SUBS):
            sector = (band_pos ^ low) & (SUBS - 1)
            rows = pl.ds(pl.multiple_of(sector * FIRST_SIDE, 8), FIRST_SIDE)
            even, odd = acc[0, rows, :] * scale, acc[1, rows, :] * scale
            out = outs[upper * SUBS + low]
            width = out.shape[1]
            pieces = even.shape[1] // width
            tails = []
            for piece in range(pieces):
                lanes = slice(piece * width, (piece + 1) * width)
                at = piece * MAIN
                out[at : at + MAIN_SIDE, :] = even[:MAIN_SIDE, lanes].astype(out.dtype)
                out[at + MAIN_SIDE : at + MAIN, :] = odd[:MAIN_SIDE, lanes].astype(out.dtype)
                for side in (even, odd):
                    tails.append(side[MAIN_SIDE : MAIN_SIDE + TAIL_SIDE, lanes])
            out[pieces * MAIN :, :] = jnp.concatenate(tails, axis=0).astype(out.dtype)


def interp_t(taps, weights, start, rows, mixed=False):
    row_ids = lax.broadcasted_iota(jnp.int32, (rows, ANGLES), 0)
    if mixed:
        ids = row_ids - MAIN
        tail = jnp.where(ids < TAIL_SIDE, 2 * ids, 2 * (ids - TAIL_SIDE) + 1) + MAIN
        ids = row_ids - MAIN_SIDE
        main = jnp.where(ids < 0, 2 * row_ids, 2 * ids + 1)
        row_ids = jnp.where(row_ids < MAIN, main, tail)
        row_ids = jnp.where(row_ids < FIRST, row_ids, -ANGLES)
    row_ids += start
    total = jnp.zeros((rows, ANGLES), jnp.float32)
    for s in range(taps.shape[0]):
        total += jnp.where(row_ids == taps[s : s + 1, :], weights[s : s + 1, :], 0.0)
    return total


def phase_rows(cos_ref, sin_ref, shift, first, count, sign):
    freqs = cos_ref.shape[1]
    ranges = (
        (lax.broadcasted_iota(jnp.int32, (1, freqs), 1) + freqs).astype(jnp.float32)
        * (2.0 * math.pi / freqs)
        * shift
    )
    groups = count // 8
    coarse_ids = lax.broadcasted_iota(jnp.int32, (groups, 1), 0) * 8 + first
    coarse = ((coarse_ids.astype(jnp.float32) + 0.5) / (2.0 * ANGLES) - 0.5) * ranges
    fine_ids = lax.broadcasted_iota(jnp.int32, (8, 1), 0)
    fine = (fine_ids.astype(jnp.float32) / (2.0 * ANGLES)) * ranges
    coarse_cos, coarse_sin = jnp.cos(coarse) * ROOT_HALF, jnp.sin(coarse) * ROOT_HALF
    fine_cos, fine_sin = jnp.cos(fine), jnp.sin(fine)
    for group in range(groups):
        c, s = coarse_cos[group : group + 1], coarse_sin[group : group + 1]
        cos_ref[group * 8 : group * 8 + 8, :] = c * fine_cos - s * fine_sin
        sin_ref[group * 8 : group * 8 + 8, :] = sign * (s * fine_cos + c * fine_sin)


def table_kernel(
    shifts, taps, weights, ranges,
    range_out, m0, m1, m2, m3, m4, c0, s0, c1, s1, c2, s2, c3, s3, c4, s4, turned,
):
    band_pos, grp_pos = lax.axis_index("band"), lax.axis_index("grp")
    h0, h1, h2 = band_pos & 1, band_pos >> 1 & 1, band_pos >> 2 & 1
    h3, h4 = grp_pos & 1, grp_pos >> 1 & 1
    count = ranges.shape[0]
    depth = ranges.shape[1]
    for k in range(count):
        range_out[k * depth : (k + 1) * depth, :] = ranges[band_pos ^ k]

    def fill(out, level, half, start, rows, first, count, row=0):
        turned[:, :rows] = interp_t(taps[level, half], weights[level, half], start, rows).T
        out[row : row + count, :rows] = turned[pl.ds(first, count), :rows].astype(jnp.bfloat16)

    first_start = FIRST_STARTS[0]
    for combo in range(1, len(FIRST_STARTS)):
        first_start = jnp.where(h1 + 2 * h2 == combo, FIRST_STARTS[combo], first_start)
    wide1 = pl.multiple_of(h1 * HALF + h2 * WIDE_STEP, 16)
    rows = MAIN + TAIL_PAD
    turned[:, :rows] = interp_t(taps[0, h0], weights[0, h0], first_start, rows, True).T
    window = turned[pl.ds(wide1, WIDE), :rows].astype(jnp.bfloat16)
    main, tail = window[:, :MAIN], window[:, MAIN:]
    for at, sign in ((0, 1), (WIDE, -1)):
        m0[at : at + WIDE, :MAIN] = main
        m0[at : at + WIDE, MAIN : 2 * MAIN] = sign * main
        m0[at : at + WIDE, 2 * MAIN : 2 * MAIN + TAIL_PAD] = tail
        m0[at : at + WIDE, 2 * MAIN + TAIL_PAD :] = sign * tail
    phase_rows(c0, s0, shifts[0], h0 * ANGLES + wide1, WIDE, 1.0)

    half2 = pl.multiple_of(h2 * HALF, HALF)
    fill(m1, 1, h1, h2 * WIDE_STEP, WIDE, half2, HALF)
    phase_rows(c1, s1, shifts[1], h1 * ANGLES + half2, HALF, 1.0)

    turned[...] = interp_t(taps[2, h2], weights[2, h2], 0, HALF).T
    for k in range(MATES):
        mate = grp_pos ^ k
        at = pl.multiple_of((mate & 1) * HALF + (mate >> 1 & 1) * SENT_STEP, 8)
        m2[k * SENT : (k + 1) * SENT, :] = turned[pl.ds(at, SENT), :].astype(jnp.bfloat16)
        phase_rows(c2.at[k], s2.at[k], shifts[2], h2 * ANGLES + at, SENT, 1.0)

    half4 = pl.multiple_of(h4 * HALF, HALF)
    fill(m3, 3, h3, h4 * SENT_STEP, SENT, half4, HALF)
    sign3 = (1 - 2 * h3).astype(jnp.float32)
    phase_rows(c3, s3, shifts[3], h3 * ANGLES + half4, HALF, sign3)
    fill(m4, 4, h4, 0, HALF, 0, ANGLES)
    sign4 = (1 - 2 * h4).astype(jnp.float32)
    phase_rows(c4, s4, shifts[4], h4 * ANGLES, ANGLES, sign4)


def send_order(count):
    return [6, 7, 5, 3, 4, 2, 1, 0] if count == SUBS else list(range(count - 1, -1, -1))


def dot(left, right):
    return jnp.dot(left, right, preferred_element_type=jnp.float32)


def turn(out, rows, total, diff, cosine, sine):
    freqs = cosine.shape[1]
    out[rows, :freqs] = (cosine * total[:, :freqs] - sine * diff[:, freqs:]).astype(out.dtype)
    out[rows, freqs:] = (cosine * total[:, freqs:] + sine * diff[:, :freqs]).astype(out.dtype)


def band_kernel(*refs, sources):
    order = send_order(sources)
    blocks = [refs[order.index(k)] for k in range(sources)]
    ranges, m0, m1, m2, c0, s0, c1, s1, c2, s2 = refs[sources : sources + 10]
    outs = refs[sources + 10 : sources + 10 + MATES]
    wide, sub0, sub1, sub2 = refs[sources + 10 + MATES :]
    depth = ranges.shape[0] // sources
    freqs = c0.shape[1]
    scale = 1.0 / math.sqrt(freqs)
    width = blocks[0].shape[1]
    pieces = blocks[0].shape[0] // FIRST
    tails = SUBS * MAIN
    wide[tails:, :] = jnp.zeros((SUBS * TAIL_PAD, wide.shape[1]), wide.dtype)
    for t in range(SUBS):
        piece, at = divmod(t * depth, width)
        for k in range(sources):
            lanes = slice(k * depth, (k + 1) * depth)
            block = blocks[k]
            wide[t * MAIN : (t + 1) * MAIN, lanes] = block[
                piece * MAIN : (piece + 1) * MAIN, at : at + depth
            ]
            row = tails + t * TAIL_PAD
            start = pieces * MAIN + piece * TAIL
            wide[row : row + TAIL, lanes] = block[start : start + TAIL, at : at + depth]
    sub0[...] = (dot(wide[...], ranges[...]) * scale).astype(sub0.dtype)
    for p in range(SUBS // 2):
        main = sub0[2 * p * MAIN : 2 * (p + 1) * MAIN, :]
        tail = sub0[tails + 2 * p * TAIL_PAD : tails + 2 * (p + 1) * TAIL_PAD, :]
        both = dot(m0[...], jnp.concatenate([main, tail], axis=0))
        turn(sub1, slice(p * WIDE, (p + 1) * WIDE), both[:WIDE], both[WIDE:], c0[...], s0[...])
    for p in range(SUBS // 4):
        low = sub1[2 * p * WIDE : (2 * p + 1) * WIDE, :]
        high = sub1[(2 * p + 1) * WIDE : (2 * p + 2) * WIDE, :]
        rows = slice(p * HALF, (p + 1) * HALF)
        turn(sub2, rows, dot(m1[...], low + high), dot(m1[...], low - high), c1[...], s1[...])
    low, high = sub2[:HALF, :], sub2[HALF:, :]
    total, diff = low + high, low - high
    total, diff = dot(m2[...], total), dot(m2[...], diff)
    for k in range(MATES):
        rows = slice(k * SENT, (k + 1) * SENT)
        turn(outs[k], slice(None), total[rows], diff[rows], c2[k], s2[k])


def own_kernel(along, own, m3, m4, c3, s3, part, sub4):
    low, high = own[...], along[...]
    turn(sub4, slice(None), dot(m3[...], low + high), dot(m3[...], low - high), c3[...], s3[...])
    part[...] = dot(m4[...], sub4[...])


def grp_kernel(across, both, part, m3, m4, c3, s3, c4, s4, out_far, sub4, out, sems):
    freqs = c3.shape[1]
    low, high = across[...], both[...]
    turn(sub4, slice(None), dot(m3[...], low + high), dot(m3[...], low - high), c3[...], s3[...])
    pieces = sems.shape[0]
    count = out.shape[1] // pieces
    copies = []
    for piece in range(pieces):
        rows = slice(piece * count, (piece + 1) * count)
        low = part[rows, :]
        high = dot(m4[rows, :], sub4[...])
        total, diff = low + high, low - high
        cosine, sine = c4[rows, :], s4[rows, :]
        out[0, rows, :] = (cosine * total[:, :freqs] - sine * diff[:, freqs:]).astype(out.dtype)
        out[1, rows, :] = (cosine * total[:, freqs:] + sine * diff[:, :freqs]).astype(out.dtype)
        copy = pltpu.make_async_copy(
            out.at[:, rows, :], out_far.at[:, rows, :], sems.at[piece]
        )
        copy.start()
        copies.append(copy)
    for copy in copies:
        copy.wait()


VMEM = pl.BlockSpec(memory_space=pltpu.VMEM)
FAR = pl.BlockSpec(memory_space=pltpu.HBM)
SMEM = pl.BlockSpec(memory_space=pltpu.SMEM)
PARAMS = pltpu.CompilerParams(vmem_limit_bytes=48 * 1024 * 1024)
BEAM_PARAMS = pltpu.CompilerParams(vmem_limit_bytes=55687168)


def swapped(block, axis, mask):
    count = lax.axis_size(axis)
    return lax.ppermute(block, axis, [(low, low ^ mask) for low in range(count)])


def on_device(raw, taps, weights, shifts):
    n_band = lax.axis_size("band")
    freqs = raw.shape[1]
    freq_count = freqs * n_band
    pulses = raw.shape[2] // n_band
    bf16, f32 = jnp.bfloat16, jnp.float32
    shape = jax.ShapeDtypeStruct
    lanes = SUBS * 2 * freqs
    pieces = max(1, lanes // 128)

    table = jnp.asarray(beam_rows(pulses))
    beams = pl.pallas_call(
        functools.partial(beam_kernel, pulses=pulses),
        out_shape=[shape((FIRST * pieces, lanes // pieces), bf16)] * n_band,
        in_specs=[FAR, FAR],
        out_specs=[VMEM] * n_band,
        scratch_shapes=[
            pltpu.VMEM(raw.shape, bf16),
            pltpu.VMEM(table.shape, bf16),
            pltpu.VMEM((2, lanes, pulses), bf16),
            pltpu.VMEM((2, SUBS * FIRST_SIDE, lanes), f32),
            pltpu.SemaphoreType.DMA,
            pltpu.SemaphoreType.DMA,
        ],
        compiler_params=BEAM_PARAMS,
        cost_estimate=pl.CostEstimate(
            flops=2 * SUBS * FIRST * pulses * lanes, bytes_accessed=1 << 21, transcendentals=0
        ),
        name="beam",
    )(raw, table)

    wide2 = 2 * freq_count
    tables = pl.pallas_call(
        table_kernel,
        out_shape=[
            shape((wide2, wide2), bf16),
            shape((2 * WIDE, 2 * (MAIN + TAIL_PAD)), bf16),
            shape((HALF, WIDE), bf16),
            shape((MATES * SENT, HALF), bf16),
            shape((HALF, SENT), bf16),
            shape((ANGLES, HALF), bf16),
        ]
        + [
            shape(rows + (freq_count,), f32)
            for rows in ((WIDE,), (HALF,), (MATES, SENT), (HALF,), (ANGLES,))
            for _ in range(2)
        ],
        in_specs=[SMEM, VMEM, VMEM, VMEM],
        out_specs=[VMEM] * 16,
        scratch_shapes=[pltpu.VMEM((ANGLES, HALF), f32)],
        compiler_params=PARAMS,
        cost_estimate=pl.CostEstimate(
            flops=1 << 24, bytes_accessed=1 << 23, transcendentals=1 << 18
        ),
        name="tables",
    )(shifts, taps, weights, jnp.asarray(range_rows(freq_count, freqs)))
    ranges, m0, m1, m2, m3, m4, c0, s0, c1, s1, c2, s2, c3, s3, c4, s4 = tables

    blocks = [swapped(beams[k], "band", k) if k else beams[k] for k in send_order(n_band)]
    pieces = pl.pallas_call(
        functools.partial(band_kernel, sources=n_band),
        out_shape=[shape((SENT, wide2), bf16)] * MATES,
        in_specs=[VMEM] * (n_band + 10),
        out_specs=[VMEM] * MATES,
        scratch_shapes=[
            pltpu.VMEM((SUBS * (MAIN + TAIL_PAD), wide2), bf16),
            pltpu.VMEM((SUBS * (MAIN + TAIL_PAD), wide2), bf16),
            pltpu.VMEM((SUBS // 2 * WIDE, wide2), bf16),
            pltpu.VMEM((SUBS // 4 * HALF, wide2), bf16),
        ],
        compiler_params=PARAMS,
        cost_estimate=pl.CostEstimate(flops=1 << 31, bytes_accessed=1 << 22, transcendentals=0),
        name="band_merges",
    )(*blocks, ranges, m0, m1, m2, c0, s0, c1, s1, c2, s2)

    halves = [swapped(pieces[k], "grp", k) for k in range(1, MATES)] + [pieces[0]]
    along, across, both, own = halves
    part = pl.pallas_call(
        own_kernel,
        out_shape=shape((ANGLES, wide2), f32),
        in_specs=[VMEM] * 6,
        out_specs=VMEM,
        scratch_shapes=[pltpu.VMEM((HALF, wide2), bf16)],
        compiler_params=PARAMS,
        cost_estimate=pl.CostEstimate(flops=1 << 29, bytes_accessed=1 << 21, transcendentals=0),
        name="own_merge",
    )(along, own, m3, m4, c3, s3)
    return pl.pallas_call(
        grp_kernel,
        out_shape=shape((2, ANGLES, freq_count), bf16),
        in_specs=[VMEM] * 9,
        out_specs=FAR,
        scratch_shapes=[
            pltpu.VMEM((HALF, wide2), bf16),
            pltpu.VMEM((2, ANGLES, freq_count), bf16),
            pltpu.SemaphoreType.DMA((4,)),
        ],
        compiler_params=PARAMS,
        cost_estimate=pl.CostEstimate(flops=1 << 29, bytes_accessed=1 << 21, transcendentals=0),
        name="grp_merges",
    )(across, both, part, m3, m4, c3, s3, c4, s4)


def solution(mesh):
    in_specs = (P(None, "band", "grp"), P(), P(), P())
    out_specs = P(None, ("grp", "band"), None)
    return jax.shard_map(
        on_device, mesh=mesh, in_specs=in_specs, out_specs=out_specs, check_vma=False
    )
```

```python
import functools
import math

import jax
import jax.numpy as jnp
import ml_dtypes
import numpy as np
from jax import lax
from jax.experimental import pallas as pl
from jax.experimental.pallas import tpu as pltpu
from jax.sharding import PartitionSpec as P

ANGLES = 512
HALF = ANGLES // 2
BAND_LEVELS = 3
GRP_LEVELS = 2
LEVELS = BAND_LEVELS + GRP_LEVELS
SUBS = 1 << BAND_LEVELS
MATES = 1 << GRP_LEVELS
ROOT_HALF = 0.7071067811865476


def up_to(value, unit):
    return -(-value // unit) * unit


def rows_read(low, high):
    return max(0, low // 2 - 1), min(HALF - 1, (high + 1) // 2 + 2)


WIDE = up_to(rows_read(0, HALF - 1)[1] + 1, 16)
WIDE_STEP = HALF - WIDE
SENT = up_to(rows_read(0, HALF - 1)[1] + 1, 4)
SENT_STEP = HALF - SENT
BULK = SENT // 16 * 16
REST = SENT - BULK
SENT_PAD = BULK + 2 * REST


def first_windows():
    spans = []
    for h2 in (0, 1):
        low, high = rows_read(h2 * HALF, h2 * HALF + HALF - 1)
        for h1 in (0, 1):
            spans.append(rows_read(h1 * HALF + low, h1 * HALF + high))
    rows = up_to(max(high - low + 1 + low % 2 for low, high in spans), 2)
    return [min(low - low % 2, HALF - rows) for low, high in spans], rows


FIRST_STARTS, FIRST = first_windows()
CLASSES = 4
CLASS_MAIN = FIRST // (16 * CLASSES) * 16
MAIN = CLASSES * CLASS_MAIN
CLASS_ROWS = [len(range(u, FIRST, CLASSES)) for u in range(CLASSES)]
CLASS_PAD = up_to(max(CLASS_ROWS), 8)
TAIL_IDS = [CLASSES * m + u for u in range(CLASSES) for m in range(CLASS_MAIN, CLASS_ROWS[u])]
TAIL = len(TAIL_IDS)
TAIL_PAD = up_to(TAIL, 8)


def beam_rows(pulses):
    pulse_ids = np.arange(pulses // CLASSES)
    table = np.zeros((CLASSES, SUBS, CLASS_PAD, 2 * len(pulse_ids)))
    for sector in range(SUBS):
        start = (sector & 1) * HALF + FIRST_STARTS[sector >> 1]
        for u in range(CLASSES):
            angle_ids = start + u + CLASSES * np.arange(CLASS_ROWS[u])
            phases = (angle_ids[:, None] * pulse_ids[None, :] % ANGLES) * (2.0 * math.pi / ANGLES)
            rows = np.concatenate([np.cos(phases), np.sin(phases)], axis=1)
            table[(start + u) % CLASSES, sector, : len(rows)] = rows
    return table.reshape(CLASSES, SUBS * CLASS_PAD, -1).astype(ml_dtypes.bfloat16)


def range_rows(freq_count, freq_local):
    ids = np.arange(freq_count)
    phases = (ids[:, None] * ids[None, :] % freq_count) * (2.0 * math.pi / freq_count)
    cosine, sine = np.cos(phases), np.sin(phases)
    table = np.stack(
        [np.concatenate([cosine, -sine], axis=1), np.concatenate([sine, cosine], axis=1)]
    )
    table = table.reshape(2, freq_count // freq_local, freq_local, 2 * freq_count)
    table = table.transpose(1, 0, 2, 3).reshape(-1, 2 * freq_local, 2 * freq_count)
    return table.astype(ml_dtypes.bfloat16)


def beam_kernel(raw_far, table_far, *refs, pulses):
    outs, (raw, table, rhs, acc, raw_sem, table_sem) = refs[:-6], refs[-6:]
    freqs = raw.shape[1]
    quarter = pulses // CLASSES
    band_pos = lax.axis_index("band")
    scale = 1.0 / math.sqrt(pulses)
    raw_copy = pltpu.make_async_copy(raw_far, raw, raw_sem)
    raw_copy.start()
    table_copy = pltpu.make_async_copy(table_far, table, table_sem)
    table_copy.start()
    raw_copy.wait()
    for upper in range(len(outs) // SUBS):
        block = band_pos // SUBS ^ upper if len(outs) > SUBS else 0
        for t in range(SUBS):
            at = pl.multiple_of((block * SUBS + t) * pulses, pulses)
            row = t * 2 * freqs
            x0, x1, x2, x3 = (
                raw[:, :, pl.ds(at + j * quarter, quarter)].astype(jnp.float32)
                for j in range(CLASSES)
            )
            even, odd, even_diff, odd_diff = x0 + x2, x1 + x3, x0 - x2, x1 - x3
            for u, (real, imag) in enumerate(
                (
                    (even[0] + odd[0], even[1] + odd[1]),
                    (even_diff[0] + odd_diff[1], even_diff[1] - odd_diff[0]),
                    (even[0] - odd[0], even[1] - odd[1]),
                    (even_diff[0] - odd_diff[1], even_diff[1] + odd_diff[0]),
                )
            ):
                real, imag = real.astype(rhs.dtype), imag.astype(rhs.dtype)
                rhs[u, row : row + freqs, :quarter] = real
                rhs[u, row : row + freqs, quarter:] = imag
                rhs[u, row + freqs : row + 2 * freqs, :quarter] = imag
                rhs[u, row + freqs : row + 2 * freqs, quarter:] = -real
        if upper == 0:
            table_copy.wait()
        for u in range(CLASSES):
            acc[u] = lax.dot_general(
                table[u],
                rhs[u],
                (((1,), (1,)), ((), ())),
                preferred_element_type=jnp.float32,
            )
        for low in range(SUBS):
            sector = (band_pos ^ low) & (SUBS - 1)
            rows = pl.ds(pl.multiple_of(sector * CLASS_PAD, 8), CLASS_PAD)
            shift = FIRST_STARTS[0] % CLASSES
            for combo in range(1, len(FIRST_STARTS)):
                shift = jnp.where(sector >> 1 == combo, FIRST_STARTS[combo] % CLASSES, shift)
            classes = [
                acc[(shift + u) & (CLASSES - 1), rows, :] * scale for u in range(CLASSES)
            ]
            out = outs[upper * SUBS + low]
            width = out.shape[1]
            pieces = acc.shape[2] // width
            tails = []
            for piece in range(pieces):
                lanes = slice(piece * width, (piece + 1) * width)
                for u, values in enumerate(classes):
                    at = piece * MAIN + u * CLASS_MAIN
                    out[at : at + CLASS_MAIN, :] = values[:CLASS_MAIN, lanes].astype(out.dtype)
                    tails.append(values[CLASS_MAIN : CLASS_ROWS[u], lanes])
            out[pieces * MAIN :, :] = jnp.concatenate(tails, axis=0).astype(out.dtype)


def interp_t(taps, weights, start, rows, mixed=False):
    row_ids = lax.broadcasted_iota(jnp.int32, (rows, ANGLES), 0)
    if mixed:
        ids = row_ids % CLASS_MAIN * CLASSES + row_ids // CLASS_MAIN
        for place in range(TAIL_PAD):
            value = TAIL_IDS[place] if place < TAIL else -ANGLES
            ids = jnp.where(row_ids == MAIN + place, value, ids)
        row_ids = ids
    row_ids += start
    total = jnp.zeros((rows, ANGLES), jnp.float32)
    for s in range(taps.shape[0]):
        total += jnp.where(row_ids == taps[s : s + 1, :], weights[s : s + 1, :], 0.0)
    return total


def phase_rows(cos_ref, sin_ref, shift, first, count, sign):
    freqs = cos_ref.shape[1]
    ranges = (
        (lax.broadcasted_iota(jnp.int32, (1, freqs), 1) + freqs).astype(jnp.float32)
        * (2.0 * math.pi / freqs)
        * shift
    )
    def turns(start, step, count):
        ids = lax.broadcasted_iota(jnp.int32, (count, 1), 0) * step + start
        angle = ids.astype(jnp.float32) / (2.0 * ANGLES) * ranges
        return jnp.cos(angle), jnp.sin(angle)

    def times(left, right):
        return left[0] * right[0] - left[1] * right[1], left[0] * right[1] + left[1] * right[0]

    offset = (0.5 / (2.0 * ANGLES) - 0.5) * ranges
    offset = (jnp.cos(offset) * ROOT_HALF, jnp.sin(offset) * ROOT_HALF)
    coarse = times(turns(first, 64, 8), offset)
    middle, fine = turns(0, 8, 8), turns(0, 1, 8)
    for group in range(count // 8):
        if group % 8 == 0:
            a = group // 8
            row = times((coarse[0][a : a + 1], coarse[1][a : a + 1]), middle)
        b = group % 8
        cosine, sine = times((row[0][b : b + 1], row[1][b : b + 1]), fine)
        cos_ref[group * 8 : group * 8 + 8, :] = cosine
        sin_ref[group * 8 : group * 8 + 8, :] = sign * sine


def table_kernel(
    shifts, taps, weights, ranges,
    range_out, m0, m1, m2, m3, m4, c0, s0, c1, s1, c2, s2, c3, s3, c4, s4, turned,
):
    band_pos, grp_pos = lax.axis_index("band"), lax.axis_index("grp")
    h0, h1, h2 = band_pos & 1, band_pos >> 1 & 1, band_pos >> 2 & 1
    h3, h4 = grp_pos & 1, grp_pos >> 1 & 1
    count = ranges.shape[0]
    depth = ranges.shape[1]
    for k in range(count):
        range_out[k * depth : (k + 1) * depth, :] = ranges[band_pos ^ k]

    def fill(out, level, half, start, rows, first, count, row=0):
        turned[:ANGLES, :rows] = interp_t(taps[level, half], weights[level, half], start, rows).T
        out[row : row + count, :rows] = turned[pl.ds(first, count), :rows].astype(jnp.bfloat16)

    first_start = FIRST_STARTS[0]
    for combo in range(1, len(FIRST_STARTS)):
        first_start = jnp.where(h1 + 2 * h2 == combo, FIRST_STARTS[combo], first_start)
    wide1 = pl.multiple_of(h1 * HALF + h2 * WIDE_STEP, 16)
    rows = MAIN + TAIL_PAD
    turned[:ANGLES, :rows] = interp_t(taps[0, h0], weights[0, h0], first_start, rows, True).T
    window = turned[pl.ds(wide1, WIDE), :rows].astype(jnp.bfloat16)
    main, tail = window[:, :MAIN], window[:, MAIN:]
    for at, sign in ((0, 1), (WIDE, -1)):
        m0[at : at + WIDE, :MAIN] = main
        m0[at : at + WIDE, MAIN : 2 * MAIN] = sign * main
        m0[at : at + WIDE, 2 * MAIN : 2 * MAIN + TAIL_PAD] = tail
        m0[at : at + WIDE, 2 * MAIN + TAIL_PAD :] = sign * tail
    phase_rows(c0, s0, shifts[0], h0 * ANGLES + wide1, WIDE, 1.0)

    half2 = pl.multiple_of(h2 * HALF, HALF)
    fill(m1, 1, h1, h2 * WIDE_STEP, WIDE, half2, HALF)
    phase_rows(c1, s1, shifts[1], h1 * ANGLES + half2, HALF, 1.0)

    turned[:ANGLES, :] = interp_t(taps[2, h2], weights[2, h2], 0, HALF).T
    turned[ANGLES:, :] = jnp.zeros((turned.shape[0] - ANGLES, HALF), jnp.float32)
    for k in range(MATES):
        mate = grp_pos ^ k
        half, side = mate & 1, mate >> 1 & 1
        rows = turned[pl.ds(pl.multiple_of(half * HALF, HALF), SENT_STEP + SENT_PAD), :]
        window = jnp.where(side == 1, rows[SENT_STEP:], rows[:SENT_PAD])
        m2[k * SENT_PAD : (k + 1) * SENT_PAD, :] = window.astype(jnp.bfloat16)
        first = h2 * ANGLES + half * HALF + side * SENT_STEP
        phase_rows(c2.at[k], s2.at[k], shifts[2], first, SENT_PAD, 1.0)

    half4 = pl.multiple_of(h4 * HALF, HALF)
    turned[:ANGLES, :SENT_PAD] = interp_t(taps[3, h3], weights[3, h3], h4 * SENT_STEP, SENT_PAD).T
    window = turned[pl.ds(half4, HALF), :SENT_PAD].astype(jnp.bfloat16)
    nothing = jnp.zeros((HALF, REST), jnp.bfloat16)
    for part in (0, 1):
        m3[part, :, :BULK] = window[:, :BULK]
        tail = BULK + part * REST
        m3[part, :, tail : tail + REST] = window[:, BULK:SENT]
        tail = BULK + (1 - part) * REST
        m3[part, :, tail : tail + REST] = nothing
    sign3 = (1 - 2 * h3).astype(jnp.float32)
    phase_rows(c3, s3, shifts[3], h3 * ANGLES + half4, HALF, sign3)
    fill(m4, 4, h4, 0, HALF, 0, ANGLES)
    sign4 = (1 - 2 * h4).astype(jnp.float32)
    phase_rows(c4, s4, shifts[4], h4 * ANGLES, ANGLES, sign4)


def send_order(count):
    return [6, 7, 5, 3, 4, 2, 1, 0] if count == SUBS else list(range(count - 1, -1, -1))


def dot(left, right):
    return jnp.dot(left, right, preferred_element_type=jnp.float32)


def turned_pair(total, diff, cosine, sine):
    freqs = cosine.shape[1]
    real = cosine * total[:, :freqs] - sine * diff[:, freqs:]
    imag = cosine * total[:, freqs:] + sine * diff[:, :freqs]
    return real, imag


def turn(out, rows, total, diff, cosine, sine):
    freqs = cosine.shape[1]
    real, imag = turned_pair(total, diff, cosine, sine)
    out[rows, :freqs] = real.astype(out.dtype)
    out[rows, freqs:] = imag.astype(out.dtype)


def merge_sent(out, low, high, m3, cosine, sine):
    freqs = cosine.shape[1]
    sides = []
    for mixed in (low + high, low - high):
        tail = mixed[2 * BULK :]
        for part in (0, 1):
            rows = jnp.concatenate([mixed[part * BULK : (part + 1) * BULK], tail], axis=0)
            sides.append(dot(m3[part], rows))
    total_real, total_imag, diff_real, diff_imag = sides
    out[:, :freqs] = (cosine * total_real - sine * diff_imag).astype(out.dtype)
    out[:, freqs:] = (cosine * total_imag + sine * diff_real).astype(out.dtype)


def band_kernel(*refs, sources):
    order = send_order(sources)
    blocks = [refs[order.index(k)] for k in range(sources)]
    ranges, m0, m1, m2, c0, s0, c1, s1, c2, s2 = refs[sources : sources + 10]
    outs = refs[sources + 10 : sources + 10 + MATES]
    wide, sub0, sub1, sub2 = refs[sources + 10 + MATES :]
    depth = ranges.shape[0] // sources
    freqs = c0.shape[1]
    scale = 1.0 / math.sqrt(freqs)
    width = blocks[0].shape[1]
    pieces = blocks[0].shape[0] // FIRST
    tails = SUBS * MAIN
    wide[tails:, :] = jnp.zeros((SUBS * TAIL_PAD, wide.shape[1]), wide.dtype)
    for t in range(SUBS):
        piece, at = divmod(t * depth, width)
        for k in range(sources):
            lanes = slice(k * depth, (k + 1) * depth)
            block = blocks[k]
            wide[t * MAIN : (t + 1) * MAIN, lanes] = block[
                piece * MAIN : (piece + 1) * MAIN, at : at + depth
            ]
            row = tails + t * TAIL_PAD
            start = pieces * MAIN + piece * TAIL
            wide[row : row + TAIL, lanes] = block[start : start + TAIL, at : at + depth]
    sub0[...] = (dot(wide[...], ranges[...]) * scale).astype(sub0.dtype)
    for p in range(SUBS // 2):
        main = sub0[2 * p * MAIN : 2 * (p + 1) * MAIN, :]
        tail = sub0[tails + 2 * p * TAIL_PAD : tails + 2 * (p + 1) * TAIL_PAD, :]
        both = dot(m0[...], jnp.concatenate([main, tail], axis=0))
        turn(sub1, slice(p * WIDE, (p + 1) * WIDE), both[:WIDE], both[WIDE:], c0[...], s0[...])
    for p in range(SUBS // 4):
        low = sub1[2 * p * WIDE : (2 * p + 1) * WIDE, :]
        high = sub1[(2 * p + 1) * WIDE : (2 * p + 2) * WIDE, :]
        rows = slice(p * HALF, (p + 1) * HALF)
        turn(sub2, rows, dot(m1[...], low + high), dot(m1[...], low - high), c1[...], s1[...])
    low, high = sub2[:HALF, :], sub2[HALF:, :]
    total, diff = low + high, low - high
    total, diff = dot(m2[...], total), dot(m2[...], diff)
    for k in range(MATES):
        rows = slice(k * SENT_PAD, (k + 1) * SENT_PAD)
        real, imag = turned_pair(total[rows], diff[rows], c2[k], s2[k])
        for part, rows in enumerate((real.astype(sub2.dtype), imag.astype(sub2.dtype))):
            outs[k][part * BULK : (part + 1) * BULK, :] = rows[:BULK]
            tail = 2 * BULK + part * REST
            outs[k][tail : tail + REST, :] = rows[BULK:SENT]


def own_kernel(along, own, m3, m4, c3, s3, part, sub4):
    merge_sent(sub4, own[...], along[...], m3, c3[...], s3[...])
    part[...] = dot(m4[...], sub4[...])


def grp_kernel(across, both, part, m3, m4, c3, s3, c4, s4, out_far, sub4, out, sems):
    freqs = c3.shape[1]
    merge_sent(sub4, across[...], both[...], m3, c3[...], s3[...])
    pieces = sems.shape[0]
    count = out.shape[1] // pieces
    copies = []
    for piece in range(pieces):
        rows = slice(piece * count, (piece + 1) * count)
        low = part[rows, :]
        high = dot(m4[rows, :], sub4[...])
        total, diff = low + high, low - high
        cosine, sine = c4[rows, :], s4[rows, :]
        out[0, rows, :] = (cosine * total[:, :freqs] - sine * diff[:, freqs:]).astype(out.dtype)
        out[1, rows, :] = (cosine * total[:, freqs:] + sine * diff[:, :freqs]).astype(out.dtype)
        copy = pltpu.make_async_copy(
            out.at[:, rows, :], out_far.at[:, rows, :], sems.at[piece]
        )
        copy.start()
        copies.append(copy)
    for copy in copies:
        copy.wait()


VMEM = pl.BlockSpec(memory_space=pltpu.VMEM)
FAR = pl.BlockSpec(memory_space=pltpu.HBM)
SMEM = pl.BlockSpec(memory_space=pltpu.SMEM)
PARAMS = pltpu.CompilerParams(vmem_limit_bytes=48 * 1024 * 1024)
BEAM_PARAMS = pltpu.CompilerParams(vmem_limit_bytes=55687168)


def swapped(block, axis, mask):
    count = lax.axis_size(axis)
    return lax.ppermute(block, axis, [(low, low ^ mask) for low in range(count)])


def on_device(raw, taps, weights, shifts):
    n_band = lax.axis_size("band")
    freqs = raw.shape[1]
    freq_count = freqs * n_band
    pulses = raw.shape[2] // n_band
    bf16, f32 = jnp.bfloat16, jnp.float32
    shape = jax.ShapeDtypeStruct
    lanes = SUBS * 2 * freqs
    pieces = max(1, lanes // 128)

    table = jnp.asarray(beam_rows(pulses))
    beams = pl.pallas_call(
        functools.partial(beam_kernel, pulses=pulses),
        out_shape=[shape((FIRST * pieces, lanes // pieces), bf16)] * n_band,
        in_specs=[FAR, FAR],
        out_specs=[VMEM] * n_band,
        scratch_shapes=[
            pltpu.VMEM(raw.shape, bf16),
            pltpu.VMEM(table.shape, bf16),
            pltpu.VMEM((CLASSES, lanes, 2 * pulses // CLASSES), bf16),
            pltpu.VMEM((CLASSES, SUBS * CLASS_PAD, lanes), f32),
            pltpu.SemaphoreType.DMA,
            pltpu.SemaphoreType.DMA,
        ],
        compiler_params=BEAM_PARAMS,
        cost_estimate=pl.CostEstimate(
            flops=SUBS * FIRST * pulses * lanes, bytes_accessed=1 << 21, transcendentals=0
        ),
        name="beam",
    )(raw, table)

    wide2 = 2 * freq_count
    tables = pl.pallas_call(
        table_kernel,
        out_shape=[
            shape((wide2, wide2), bf16),
            shape((2 * WIDE, 2 * (MAIN + TAIL_PAD)), bf16),
            shape((HALF, WIDE), bf16),
            shape((MATES * SENT_PAD, HALF), bf16),
            shape((2, HALF, SENT_PAD), bf16),
            shape((ANGLES, HALF), bf16),
        ]
        + [
            shape(rows + (freq_count,), f32)
            for rows in ((WIDE,), (HALF,), (MATES, SENT_PAD), (HALF,), (ANGLES,))
            for _ in range(2)
        ],
        in_specs=[SMEM, VMEM, VMEM, VMEM],
        out_specs=[VMEM] * 16,
        scratch_shapes=[pltpu.VMEM((ANGLES + 2 * REST, HALF), f32)],
        compiler_params=PARAMS,
        cost_estimate=pl.CostEstimate(
            flops=1 << 24, bytes_accessed=1 << 23, transcendentals=1 << 18
        ),
        name="tables",
    )(shifts, taps, weights, jnp.asarray(range_rows(freq_count, freqs)))
    ranges, m0, m1, m2, m3, m4, c0, s0, c1, s1, c2, s2, c3, s3, c4, s4 = tables

    blocks = [swapped(beams[k], "band", k) if k else beams[k] for k in send_order(n_band)]
    pieces = pl.pallas_call(
        functools.partial(band_kernel, sources=n_band),
        out_shape=[shape((2 * SENT, freq_count), bf16)] * MATES,
        in_specs=[VMEM] * (n_band + 10),
        out_specs=[VMEM] * MATES,
        scratch_shapes=[
            pltpu.VMEM((SUBS * (MAIN + TAIL_PAD), wide2), bf16),
            pltpu.VMEM((SUBS * (MAIN + TAIL_PAD), wide2), bf16),
            pltpu.VMEM((SUBS // 2 * WIDE, wide2), bf16),
            pltpu.VMEM((SUBS // 4 * HALF, wide2), bf16),
        ],
        compiler_params=PARAMS,
        cost_estimate=pl.CostEstimate(flops=1 << 31, bytes_accessed=1 << 22, transcendentals=0),
        name="band_merges",
    )(*blocks, ranges, m0, m1, m2, c0, s0, c1, s1, c2, s2)

    halves = [swapped(pieces[k], "grp", k) for k in range(1, MATES)] + [pieces[0]]
    along, across, both, own = halves
    part = pl.pallas_call(
        own_kernel,
        out_shape=shape((ANGLES, wide2), f32),
        in_specs=[VMEM] * 6,
        out_specs=VMEM,
        scratch_shapes=[pltpu.VMEM((HALF, wide2), bf16)],
        compiler_params=PARAMS,
        cost_estimate=pl.CostEstimate(flops=1 << 29, bytes_accessed=1 << 21, transcendentals=0),
        name="own_merge",
    )(along, own, m3, m4, c3, s3)
    return pl.pallas_call(
        grp_kernel,
        out_shape=shape((2, ANGLES, freq_count), bf16),
        in_specs=[VMEM] * 9,
        out_specs=FAR,
        scratch_shapes=[
            pltpu.VMEM((HALF, wide2), bf16),
            pltpu.VMEM((2, ANGLES, freq_count), bf16),
            pltpu.SemaphoreType.DMA((4,)),
        ],
        compiler_params=PARAMS,
        cost_estimate=pl.CostEstimate(flops=1 << 29, bytes_accessed=1 << 21, transcendentals=0),
        name="grp_merges",
    )(across, both, part, m3, m4, c3, s3, c4, s4)


def solution(mesh):
    in_specs = (P(None, "band", "grp"), P(), P(), P())
    out_specs = P(None, ("grp", "band"), None)
    return jax.shard_map(
        on_device, mesh=mesh, in_specs=in_specs, out_specs=out_specs, check_vma=False
    )
```

```python
import functools
import math

import jax
import jax.numpy as jnp
import ml_dtypes
import numpy as np
from jax import lax
from jax.experimental import pallas as pl
from jax.experimental.pallas import tpu as pltpu
from jax.sharding import PartitionSpec as P

ANGLES = 512
HALF = ANGLES // 2
BAND_LEVELS = 3
GRP_LEVELS = 2
LEVELS = BAND_LEVELS + GRP_LEVELS
SUBS = 1 << BAND_LEVELS
MATES = 1 << GRP_LEVELS
ROOT_HALF = 0.7071067811865476


def up_to(value, unit):
    return -(-value // unit) * unit


def rows_read(low, high):
    return max(0, low // 2 - 1), min(HALF - 1, (high + 1) // 2 + 2)


WIDE = up_to(rows_read(0, HALF - 1)[1] + 1, 16)
WIDE_STEP = HALF - WIDE
SENT = up_to(rows_read(0, HALF - 1)[1] + 1, 8)
SENT_STEP = HALF - SENT
BULK = SENT // 16 * 16
REST = SENT - BULK
SENT_PAD = BULK + 2 * REST


def first_windows():
    spans = []
    for h2 in (0, 1):
        low, high = rows_read(h2 * HALF, h2 * HALF + HALF - 1)
        for h1 in (0, 1):
            spans.append(rows_read(h1 * HALF + low, h1 * HALF + high))
    rows = up_to(max(high - low + 1 + low % 2 for low, high in spans), 8)
    return [min(low - low % 2, HALF - rows) for low, high in spans], rows


FIRST_STARTS, FIRST = first_windows()
CLASSES = 4
CLASS_MAIN = FIRST // (16 * CLASSES) * 16
MAIN = CLASSES * CLASS_MAIN
CLASS_ROWS = [len(range(u, FIRST, CLASSES)) for u in range(CLASSES)]
CLASS_PAD = up_to(max(CLASS_ROWS), 8)
TAIL_IDS = [CLASSES * m + u for u in range(CLASSES) for m in range(CLASS_MAIN, CLASS_ROWS[u])]
TAIL = len(TAIL_IDS)
TAIL_PAD = up_to(TAIL, 16)


def beam_rows(pulses):
    pulse_ids = np.arange(pulses // CLASSES)
    table = np.zeros((CLASSES, SUBS, CLASS_PAD, 2 * len(pulse_ids)))
    for sector in range(SUBS):
        start = (sector & 1) * HALF + FIRST_STARTS[sector >> 1]
        for u in range(CLASSES):
            angle_ids = start + u + CLASSES * np.arange(CLASS_ROWS[u])
            phases = (angle_ids[:, None] * pulse_ids[None, :] % ANGLES) * (2.0 * math.pi / ANGLES)
            rows = np.concatenate([np.cos(phases), np.sin(phases)], axis=1)
            table[(start + u) % CLASSES, sector, : len(rows)] = rows
    return table.reshape(CLASSES, SUBS * CLASS_PAD, -1).astype(ml_dtypes.bfloat16)


def range_rows(freq_count, freq_local):
    ids = np.arange(freq_count)
    phases = (ids[:, None] * ids[None, :] % freq_count) * (2.0 * math.pi / freq_count)
    cosine, sine = np.cos(phases), np.sin(phases)
    table = np.stack(
        [np.concatenate([cosine, -sine], axis=1), np.concatenate([sine, cosine], axis=1)]
    )
    table = table.reshape(2, freq_count // freq_local, freq_local, 2 * freq_count)
    table = table.transpose(1, 0, 2, 3).reshape(-1, 2 * freq_local, 2 * freq_count)
    return table.astype(ml_dtypes.bfloat16)


def beam_kernel(raw_far, table_far, *refs, pulses):
    outs, (raw, table, rhs, acc, raw_sem, table_sem) = refs[:-6], refs[-6:]
    freqs = raw.shape[1]
    quarter = pulses // CLASSES
    band_pos = lax.axis_index("band")
    scale = 1.0 / math.sqrt(pulses)
    raw_copy = pltpu.make_async_copy(raw_far, raw, raw_sem)
    raw_copy.start()
    table_copy = pltpu.make_async_copy(table_far, table, table_sem)
    table_copy.start()
    raw_copy.wait()
    for upper in range(len(outs) // SUBS):
        block = band_pos // SUBS ^ upper if len(outs) > SUBS else 0
        for t in range(SUBS):
            at = pl.multiple_of((block * SUBS + t) * pulses, pulses)
            row = t * 2 * freqs
            x0, x1, x2, x3 = (
                raw[:, :, pl.ds(at + j * quarter, quarter)].astype(jnp.float32)
                for j in range(CLASSES)
            )
            even, odd, even_diff, odd_diff = x0 + x2, x1 + x3, x0 - x2, x1 - x3
            for u, (real, imag) in enumerate(
                (
                    (even[0] + odd[0], even[1] + odd[1]),
                    (even_diff[0] + odd_diff[1], even_diff[1] - odd_diff[0]),
                    (even[0] - odd[0], even[1] - odd[1]),
                    (even_diff[0] - odd_diff[1], even_diff[1] + odd_diff[0]),
                )
            ):
                real, imag = real.astype(rhs.dtype), imag.astype(rhs.dtype)
                rhs[u, row : row + freqs, :quarter] = real
                rhs[u, row : row + freqs, quarter:] = imag
                rhs[u, row + freqs : row + 2 * freqs, :quarter] = imag
                rhs[u, row + freqs : row + 2 * freqs, quarter:] = -real
        if upper == 0:
            table_copy.wait()
        for u in range(CLASSES):
            acc[u] = lax.dot_general(
                table[u],
                rhs[u],
                (((1,), (1,)), ((), ())),
                preferred_element_type=jnp.float32,
            )
        for low in range(SUBS):
            sector = (band_pos ^ low) & (SUBS - 1)
            rows = pl.ds(pl.multiple_of(sector * CLASS_PAD, 8), CLASS_PAD)
            shift = FIRST_STARTS[0] % CLASSES
            for combo in range(1, len(FIRST_STARTS)):
                shift = jnp.where(sector >> 1 == combo, FIRST_STARTS[combo] % CLASSES, shift)
            classes = [
                acc[(shift + u) & (CLASSES - 1), rows, :] * scale for u in range(CLASSES)
            ]
            out = outs[upper * SUBS + low]
            width = out.shape[1]
            pieces = acc.shape[2] // width
            tails = []
            for piece in range(pieces):
                lanes = slice(piece * width, (piece + 1) * width)
                for u, values in enumerate(classes):
                    at = piece * MAIN + u * CLASS_MAIN
                    out[at : at + CLASS_MAIN, :] = values[:CLASS_MAIN, lanes].astype(out.dtype)
                    tails.append(values[CLASS_MAIN : CLASS_ROWS[u], lanes])
            out[pieces * MAIN :, :] = jnp.concatenate(tails, axis=0).astype(out.dtype)


def interp_t(taps, weights, start, rows, mixed=False):
    row_ids = lax.broadcasted_iota(jnp.int32, (rows, ANGLES), 0)
    if mixed:
        ids = row_ids % CLASS_MAIN * CLASSES + row_ids // CLASS_MAIN
        for place in range(TAIL_PAD):
            value = TAIL_IDS[place] if place < TAIL else -ANGLES
            ids = jnp.where(row_ids == MAIN + place, value, ids)
        row_ids = ids
    row_ids += start
    total = jnp.zeros((rows, ANGLES), jnp.float32)
    for s in range(taps.shape[0]):
        total += jnp.where(row_ids == taps[s : s + 1, :], weights[s : s + 1, :], 0.0)
    return total


def phase_rows(cos_ref, sin_ref, shift, first, count, sign):
    freqs = cos_ref.shape[1]
    ranges = (
        (lax.broadcasted_iota(jnp.int32, (1, freqs), 1) + freqs).astype(jnp.float32)
        * (2.0 * math.pi / freqs)
        * shift
    )
    def turns(start, step, count):
        ids = lax.broadcasted_iota(jnp.int32, (count, 1), 0) * step + start
        angle = ids.astype(jnp.float32) / (2.0 * ANGLES) * ranges
        return jnp.cos(angle), jnp.sin(angle)

    def times(left, right):
        return left[0] * right[0] - left[1] * right[1], left[0] * right[1] + left[1] * right[0]

    offset = (0.5 / (2.0 * ANGLES) - 0.5) * ranges
    offset = (jnp.cos(offset) * ROOT_HALF, jnp.sin(offset) * ROOT_HALF)
    coarse = times(turns(first, 64, 8), offset)
    middle, fine = turns(0, 8, 8), turns(0, 1, 8)
    for group in range(count // 8):
        if group % 8 == 0:
            a = group // 8
            row = times((coarse[0][a : a + 1], coarse[1][a : a + 1]), middle)
        b = group % 8
        cosine, sine = times((row[0][b : b + 1], row[1][b : b + 1]), fine)
        cos_ref[group * 8 : group * 8 + 8, :] = cosine
        sin_ref[group * 8 : group * 8 + 8, :] = sign * sine


def table_kernel(
    shifts, taps, weights, ranges,
    range_out, m0, m1, m2, m3, m4, c0, s0, c1, s1, c2, s2, c3, s3, c4, s4, turned,
):
    band_pos, grp_pos = lax.axis_index("band"), lax.axis_index("grp")
    h0, h1, h2 = band_pos & 1, band_pos >> 1 & 1, band_pos >> 2 & 1
    h3, h4 = grp_pos & 1, grp_pos >> 1 & 1
    count = ranges.shape[0]
    depth = ranges.shape[1]
    for k in range(count):
        range_out[k * depth : (k + 1) * depth, :] = ranges[band_pos ^ k]

    def fill(out, level, half, start, rows, first, count, row=0):
        turned[:ANGLES, :rows] = interp_t(taps[level, half], weights[level, half], start, rows).T
        out[row : row + count, :rows] = turned[pl.ds(first, count), :rows].astype(jnp.bfloat16)

    first_start = FIRST_STARTS[0]
    for combo in range(1, len(FIRST_STARTS)):
        first_start = jnp.where(h1 + 2 * h2 == combo, FIRST_STARTS[combo], first_start)
    wide1 = pl.multiple_of(h1 * HALF + h2 * WIDE_STEP, 16)
    rows = MAIN + TAIL_PAD
    turned[:ANGLES, :rows] = interp_t(taps[0, h0], weights[0, h0], first_start, rows, True).T
    window = turned[pl.ds(wide1, WIDE), :rows].astype(jnp.bfloat16)
    main, tail = window[:, :MAIN], window[:, MAIN:]
    for at, sign in ((0, 1), (WIDE, -1)):
        m0[at : at + WIDE, :MAIN] = main
        m0[at : at + WIDE, MAIN : 2 * MAIN] = sign * main
        m0[at : at + WIDE, 2 * MAIN : 2 * MAIN + TAIL_PAD] = tail
        m0[at : at + WIDE, 2 * MAIN + TAIL_PAD :] = sign * tail
    phase_rows(c0, s0, shifts[0], h0 * ANGLES + wide1, WIDE, 1.0)

    half2 = pl.multiple_of(h2 * HALF, HALF)
    fill(m1, 1, h1, h2 * WIDE_STEP, WIDE, half2, HALF)
    phase_rows(c1, s1, shifts[1], h1 * ANGLES + half2, HALF, 1.0)

    turned[:ANGLES, :] = interp_t(taps[2, h2], weights[2, h2], 0, HALF).T
    turned[ANGLES:, :] = jnp.zeros((turned.shape[0] - ANGLES, HALF), jnp.float32)
    for k in range(MATES):
        mate = grp_pos ^ k
        half, side = mate & 1, mate >> 1 & 1
        rows = turned[pl.ds(pl.multiple_of(half * HALF, HALF), SENT_STEP + SENT_PAD), :]
        window = jnp.where(side == 1, rows[SENT_STEP:], rows[:SENT_PAD])
        m2[k * SENT_PAD : (k + 1) * SENT_PAD, :] = window.astype(jnp.bfloat16)
        first = h2 * ANGLES + half * HALF + side * SENT_STEP
        phase_rows(c2.at[k], s2.at[k], shifts[2], first, SENT_PAD, 1.0)

    half4 = pl.multiple_of(h4 * HALF, HALF)
    turned[:ANGLES, :SENT_PAD] = interp_t(taps[3, h3], weights[3, h3], h4 * SENT_STEP, SENT_PAD).T
    window = turned[pl.ds(half4, HALF), :SENT_PAD].astype(jnp.bfloat16)
    nothing = jnp.zeros((HALF, REST), jnp.bfloat16)
    for part in (0, 1):
        m3[part, :, :BULK] = window[:, :BULK]
        tail = BULK + part * REST
        m3[part, :, tail : tail + REST] = window[:, BULK:SENT]
        tail = BULK + (1 - part) * REST
        m3[part, :, tail : tail + REST] = nothing
    sign3 = (1 - 2 * h3).astype(jnp.float32)
    phase_rows(c3, s3, shifts[3], h3 * ANGLES + half4, HALF, sign3)
    fill(m4, 4, h4, 0, HALF, 0, ANGLES)
    sign4 = (1 - 2 * h4).astype(jnp.float32)
    phase_rows(c4, s4, shifts[4], h4 * ANGLES, ANGLES, sign4)


def send_order(count):
    return [6, 7, 5, 3, 4, 2, 1, 0] if count == SUBS else list(range(count - 1, -1, -1))


def dot(left, right):
    return jnp.dot(left, right, preferred_element_type=jnp.float32)


def turned_pair(total, diff, cosine, sine):
    freqs = cosine.shape[1]
    real = cosine * total[:, :freqs] - sine * diff[:, freqs:]
    imag = cosine * total[:, freqs:] + sine * diff[:, :freqs]
    return real, imag


def turn(out, rows, total, diff, cosine, sine):
    freqs = cosine.shape[1]
    real, imag = turned_pair(total, diff, cosine, sine)
    out[rows, :freqs] = real.astype(out.dtype)
    out[rows, freqs:] = imag.astype(out.dtype)


def merge_sent(out, low, high, m3, cosine, sine):
    freqs = cosine.shape[1]
    sides = []
    for mixed in (low + high, low - high):
        tail = mixed[2 * BULK :]
        for part in (0, 1):
            rows = jnp.concatenate([mixed[part * BULK : (part + 1) * BULK], tail], axis=0)
            sides.append(dot(m3[part], rows))
    total_real, total_imag, diff_real, diff_imag = sides
    out[:, :freqs] = (cosine * total_real - sine * diff_imag).astype(out.dtype)
    out[:, freqs:] = (cosine * total_imag + sine * diff_real).astype(out.dtype)


def band_kernel(*refs, sources):
    order = send_order(sources)
    blocks = [refs[order.index(k)] for k in range(sources)]
    ranges, m0, m1, m2, c0, s0, c1, s1, c2, s2 = refs[sources : sources + 10]
    outs = refs[sources + 10 : sources + 10 + MATES]
    wide, sub0, sub1, sub2 = refs[sources + 10 + MATES :]
    depth = ranges.shape[0] // sources
    freqs = c0.shape[1]
    scale = 1.0 / math.sqrt(freqs)
    width = blocks[0].shape[1]
    pieces = blocks[0].shape[0] // FIRST
    tails = SUBS * MAIN
    blank = jnp.zeros((TAIL_PAD - TAIL, depth), wide.dtype)
    for k in range(sources):
        lanes = slice(k * depth, (k + 1) * depth)
        ends = blocks[k][pieces * MAIN :, :]
        for t in range(SUBS):
            piece, at = divmod(t * depth, width)
            wide[t * MAIN : (t + 1) * MAIN, lanes] = blocks[k][
                piece * MAIN : (piece + 1) * MAIN, at : at + depth
            ]
            end = ends[piece * TAIL : (piece + 1) * TAIL, at : at + depth]
            row = tails + t * TAIL_PAD
            wide[row : row + TAIL_PAD, lanes] = jnp.concatenate([end, blank], axis=0)
    sub0[...] = (dot(wide[...], ranges[...]) * scale).astype(sub0.dtype)
    for p in range(SUBS // 2):
        main = sub0[2 * p * MAIN : 2 * (p + 1) * MAIN, :]
        tail = sub0[tails + 2 * p * TAIL_PAD : tails + 2 * (p + 1) * TAIL_PAD, :]
        both = dot(m0[...], jnp.concatenate([main, tail], axis=0))
        turn(sub1, slice(p * WIDE, (p + 1) * WIDE), both[:WIDE], both[WIDE:], c0[...], s0[...])
    for p in range(SUBS // 4):
        low = sub1[2 * p * WIDE : (2 * p + 1) * WIDE, :]
        high = sub1[(2 * p + 1) * WIDE : (2 * p + 2) * WIDE, :]
        rows = slice(p * HALF, (p + 1) * HALF)
        turn(sub2, rows, dot(m1[...], low + high), dot(m1[...], low - high), c1[...], s1[...])
    low, high = sub2[:HALF, :], sub2[HALF:, :]
    total, diff = low + high, low - high
    total, diff = dot(m2[...], total), dot(m2[...], diff)
    for k in range(MATES):
        rows = slice(k * SENT_PAD, (k + 1) * SENT_PAD)
        real, imag = turned_pair(total[rows], diff[rows], c2[k], s2[k])
        outs[k][:BULK, :] = real[:BULK].astype(sub2.dtype)
        outs[k][BULK : 2 * BULK, :] = imag[:BULK].astype(sub2.dtype)
        ends = jnp.concatenate([real[BULK:SENT], imag[BULK:SENT]], axis=0)
        outs[k][2 * BULK :, :] = ends.astype(sub2.dtype)


def own_kernel(along, own, m3, m4, c3, s3, part, sub4):
    merge_sent(sub4, own[...], along[...], m3, c3[...], s3[...])
    part[...] = dot(m4[...], sub4[...])


def grp_kernel(across, both, part, m3, m4, c3, s3, c4, s4, out_far, sub4, out, sems):
    freqs = c3.shape[1]
    merge_sent(sub4, across[...], both[...], m3, c3[...], s3[...])
    pieces = sems.shape[0]
    count = out.shape[1] // pieces
    copies = []
    for piece in range(pieces):
        rows = slice(piece * count, (piece + 1) * count)
        low = part[rows, :]
        high = dot(m4[rows, :], sub4[...])
        total, diff = low + high, low - high
        cosine, sine = c4[rows, :], s4[rows, :]
        out[0, rows, :] = (cosine * total[:, :freqs] - sine * diff[:, freqs:]).astype(out.dtype)
        out[1, rows, :] = (cosine * total[:, freqs:] + sine * diff[:, :freqs]).astype(out.dtype)
        copy = pltpu.make_async_copy(
            out.at[:, rows, :], out_far.at[:, rows, :], sems.at[piece]
        )
        copy.start()
        copies.append(copy)
    for copy in copies:
        copy.wait()


VMEM = pl.BlockSpec(memory_space=pltpu.VMEM)
FAR = pl.BlockSpec(memory_space=pltpu.HBM)
SMEM = pl.BlockSpec(memory_space=pltpu.SMEM)
PARAMS = pltpu.CompilerParams(vmem_limit_bytes=48 * 1024 * 1024)
BEAM_PARAMS = pltpu.CompilerParams(vmem_limit_bytes=55687168)


def swapped(block, axis, mask):
    count = lax.axis_size(axis)
    return lax.ppermute(block, axis, [(low, low ^ mask) for low in range(count)])


def on_device(raw, taps, weights, shifts):
    n_band = lax.axis_size("band")
    freqs = raw.shape[1]
    freq_count = freqs * n_band
    pulses = raw.shape[2] // n_band
    bf16, f32 = jnp.bfloat16, jnp.float32
    shape = jax.ShapeDtypeStruct
    lanes = SUBS * 2 * freqs
    pieces = max(1, lanes // 128)

    table = jnp.asarray(beam_rows(pulses))
    beams = pl.pallas_call(
        functools.partial(beam_kernel, pulses=pulses),
        out_shape=[shape((FIRST * pieces, lanes // pieces), bf16)] * n_band,
        in_specs=[FAR, FAR],
        out_specs=[VMEM] * n_band,
        scratch_shapes=[
            pltpu.VMEM(raw.shape, bf16),
            pltpu.VMEM(table.shape, bf16),
            pltpu.VMEM((CLASSES, lanes, 2 * pulses // CLASSES), bf16),
            pltpu.VMEM((CLASSES, SUBS * CLASS_PAD, lanes), f32),
            pltpu.SemaphoreType.DMA,
            pltpu.SemaphoreType.DMA,
        ],
        compiler_params=BEAM_PARAMS,
        cost_estimate=pl.CostEstimate(
            flops=SUBS * FIRST * pulses * lanes, bytes_accessed=1 << 21, transcendentals=0
        ),
        name="beam",
    )(raw, table)

    wide2 = 2 * freq_count
    tables = pl.pallas_call(
        table_kernel,
        out_shape=[
            shape((wide2, wide2), bf16),
            shape((2 * WIDE, 2 * (MAIN + TAIL_PAD)), bf16),
            shape((HALF, WIDE), bf16),
            shape((MATES * SENT_PAD, HALF), bf16),
            shape((2, HALF, SENT_PAD), bf16),
            shape((ANGLES, HALF), bf16),
        ]
        + [
            shape(rows + (freq_count,), f32)
            for rows in ((WIDE,), (HALF,), (MATES, SENT_PAD), (HALF,), (ANGLES,))
            for _ in range(2)
        ],
        in_specs=[SMEM, VMEM, VMEM, VMEM],
        out_specs=[VMEM] * 16,
        scratch_shapes=[pltpu.VMEM((ANGLES + 2 * REST, HALF), f32)],
        compiler_params=PARAMS,
        cost_estimate=pl.CostEstimate(
            flops=1 << 24, bytes_accessed=1 << 23, transcendentals=1 << 18
        ),
        name="tables",
    )(shifts, taps, weights, jnp.asarray(range_rows(freq_count, freqs)))
    ranges, m0, m1, m2, m3, m4, c0, s0, c1, s1, c2, s2, c3, s3, c4, s4 = tables

    blocks = [swapped(beams[k], "band", k) if k else beams[k] for k in send_order(n_band)]
    pieces = pl.pallas_call(
        functools.partial(band_kernel, sources=n_band),
        out_shape=[shape((2 * SENT, freq_count), bf16)] * MATES,
        in_specs=[VMEM] * (n_band + 10),
        out_specs=[VMEM] * MATES,
        scratch_shapes=[
            pltpu.VMEM((SUBS * (MAIN + TAIL_PAD), wide2), bf16),
            pltpu.VMEM((SUBS * (MAIN + TAIL_PAD), wide2), bf16),
            pltpu.VMEM((SUBS // 2 * WIDE, wide2), bf16),
            pltpu.VMEM((SUBS // 4 * HALF, wide2), bf16),
        ],
        compiler_params=PARAMS,
        cost_estimate=pl.CostEstimate(flops=1 << 31, bytes_accessed=1 << 22, transcendentals=0),
        name="band_merges",
    )(*blocks, ranges, m0, m1, m2, c0, s0, c1, s1, c2, s2)

    halves = [swapped(pieces[k], "grp", k) for k in range(1, MATES)] + [pieces[0]]
    along, across, both, own = halves
    part = pl.pallas_call(
        own_kernel,
        out_shape=shape((ANGLES, wide2), f32),
        in_specs=[VMEM] * 6,
        out_specs=VMEM,
        scratch_shapes=[pltpu.VMEM((HALF, wide2), bf16)],
        compiler_params=PARAMS,
        cost_estimate=pl.CostEstimate(flops=1 << 29, bytes_accessed=1 << 21, transcendentals=0),
        name="own_merge",
    )(along, own, m3, m4, c3, s3)
    return pl.pallas_call(
        grp_kernel,
        out_shape=shape((2, ANGLES, freq_count), bf16),
        in_specs=[VMEM] * 9,
        out_specs=FAR,
        scratch_shapes=[
            pltpu.VMEM((HALF, wide2), bf16),
            pltpu.VMEM((2, ANGLES, freq_count), bf16),
            pltpu.SemaphoreType.DMA((4,)),
        ],
        compiler_params=PARAMS,
        cost_estimate=pl.CostEstimate(flops=1 << 29, bytes_accessed=1 << 21, transcendentals=0),
        name="grp_merges",
    )(across, both, part, m3, m4, c3, s3, c4, s4)


def solution(mesh):
    in_specs = (P(None, "band", "grp"), P(), P(), P())
    out_specs = P(None, ("grp", "band"), None)
    return jax.shard_map(
        on_device, mesh=mesh, in_specs=in_specs, out_specs=out_specs, check_vma=False
    )
```

```python
import functools
import math

import jax
import jax.numpy as jnp
import ml_dtypes
import numpy as np
from jax import lax
from jax.experimental import pallas as pl
from jax.experimental.pallas import tpu as pltpu
from jax.sharding import PartitionSpec as P

ANGLES = 512
HALF = ANGLES // 2
BAND_LEVELS = 3
GRP_LEVELS = 2
LEVELS = BAND_LEVELS + GRP_LEVELS
SUBS = 1 << BAND_LEVELS
MATES = 1 << GRP_LEVELS
ROOT_HALF = 0.7071067811865476


def up_to(value, unit):
    return -(-value // unit) * unit


def rows_read(low, high):
    return max(0, low // 2 - 1), min(HALF - 1, (high + 1) // 2 + 2)


WIDE = up_to(rows_read(0, HALF - 1)[1] + 1, 16)
WIDE_STEP = HALF - WIDE
SENT = up_to(rows_read(0, HALF - 1)[1] + 1, 8)
SENT_STEP = HALF - SENT
BULK = SENT // 16 * 16
REST = SENT - BULK
SENT_PAD = BULK + 2 * REST


def first_windows():
    spans = []
    for h2 in (0, 1):
        low, high = rows_read(h2 * HALF, h2 * HALF + HALF - 1)
        for h1 in (0, 1):
            spans.append(rows_read(h1 * HALF + low, h1 * HALF + high))
    rows = up_to(max(high - low + 1 + low % 2 for low, high in spans), 8)
    return [min(low - low % 2, HALF - rows) for low, high in spans], rows


FIRST_STARTS, FIRST = first_windows()
CLASSES = 4
CLASS_MAIN = FIRST // (16 * CLASSES) * 16
MAIN = CLASSES * CLASS_MAIN
CLASS_ROWS = [len(range(u, FIRST, CLASSES)) for u in range(CLASSES)]
CLASS_PAD = up_to(max(CLASS_ROWS), 8)
TAIL_IDS = [CLASSES * m + u for u in range(CLASSES) for m in range(CLASS_MAIN, CLASS_ROWS[u])]
TAIL = len(TAIL_IDS)
TAIL_PAD = up_to(TAIL, 16)


def beam_rows(pulses):
    pulse_ids = np.arange(pulses // CLASSES)
    table = np.zeros((CLASSES, SUBS, CLASS_PAD, 2 * len(pulse_ids)))
    for sector in range(SUBS):
        start = (sector & 1) * HALF + FIRST_STARTS[sector >> 1]
        for u in range(CLASSES):
            angle_ids = start + u + CLASSES * np.arange(CLASS_ROWS[u])
            phases = (angle_ids[:, None] * pulse_ids[None, :] % ANGLES) * (2.0 * math.pi / ANGLES)
            rows = np.concatenate([np.cos(phases), np.sin(phases)], axis=1)
            table[(start + u) % CLASSES, sector, : len(rows)] = rows
    return table.reshape(CLASSES, SUBS * CLASS_PAD, -1).astype(ml_dtypes.bfloat16)


def range_rows(freq_count, freq_local):
    ids = np.arange(freq_count)
    phases = (ids[:, None] * ids[None, :] % freq_count) * (2.0 * math.pi / freq_count)
    cosine, sine = np.cos(phases), np.sin(phases)
    table = np.stack(
        [np.concatenate([cosine, -sine], axis=1), np.concatenate([sine, cosine], axis=1)]
    )
    table = table.reshape(2, freq_count // freq_local, freq_local, 2 * freq_count)
    table = table.transpose(1, 0, 2, 3).reshape(-1, 2 * freq_local, 2 * freq_count)
    return table.astype(ml_dtypes.bfloat16)


def beam_kernel(raw_far, table_far, *refs, pulses):
    outs, (raw, table, rhs, acc, raw_sem, table_sem) = refs[:-6], refs[-6:]
    freqs = raw.shape[1]
    quarter = pulses // CLASSES
    band_pos = lax.axis_index("band")
    scale = 1.0 / math.sqrt(pulses)
    raw_copy = pltpu.make_async_copy(raw_far, raw, raw_sem)
    raw_copy.start()
    table_copy = pltpu.make_async_copy(table_far, table, table_sem)
    table_copy.start()
    raw_copy.wait()
    for upper in range(len(outs) // SUBS):
        block = band_pos // SUBS ^ upper if len(outs) > SUBS else 0
        for t in range(SUBS):
            at = pl.multiple_of((block * SUBS + t) * pulses, pulses)
            row = t * 2 * freqs
            x0, x1, x2, x3 = (
                raw[:, :, pl.ds(at + j * quarter, quarter)].astype(jnp.float32)
                for j in range(CLASSES)
            )
            even, odd, even_diff, odd_diff = x0 + x2, x1 + x3, x0 - x2, x1 - x3
            for u, (real, imag) in enumerate(
                (
                    (even[0] + odd[0], even[1] + odd[1]),
                    (even_diff[0] + odd_diff[1], even_diff[1] - odd_diff[0]),
                    (even[0] - odd[0], even[1] - odd[1]),
                    (even_diff[0] - odd_diff[1], even_diff[1] + odd_diff[0]),
                )
            ):
                real, imag = real.astype(rhs.dtype), imag.astype(rhs.dtype)
                rhs[u, row : row + freqs, :quarter] = real
                rhs[u, row : row + freqs, quarter:] = imag
                rhs[u, row + freqs : row + 2 * freqs, :quarter] = imag
                rhs[u, row + freqs : row + 2 * freqs, quarter:] = -real
        if upper == 0:
            table_copy.wait()
        for u in range(CLASSES):
            acc[u] = lax.dot_general(
                table[u],
                rhs[u],
                (((1,), (1,)), ((), ())),
                preferred_element_type=jnp.float32,
            )
        for low in range(SUBS):
            sector = (band_pos ^ low) & (SUBS - 1)
            rows = pl.ds(pl.multiple_of(sector * CLASS_PAD, 8), CLASS_PAD)
            shift = FIRST_STARTS[0] % CLASSES
            for combo in range(1, len(FIRST_STARTS)):
                shift = jnp.where(sector >> 1 == combo, FIRST_STARTS[combo] % CLASSES, shift)
            classes = [
                acc[(shift + u) & (CLASSES - 1), rows, :] * scale for u in range(CLASSES)
            ]
            out = outs[upper * SUBS + low]
            width = out.shape[1]
            pieces = acc.shape[2] // width
            tails = []
            for piece in range(pieces):
                lanes = slice(piece * width, (piece + 1) * width)
                for u, values in enumerate(classes):
                    at = piece * MAIN + u * CLASS_MAIN
                    out[at : at + CLASS_MAIN, :] = values[:CLASS_MAIN, lanes].astype(out.dtype)
                    tails.append(values[CLASS_MAIN : CLASS_ROWS[u], lanes])
            out[pieces * MAIN :, :] = jnp.concatenate(tails, axis=0).astype(out.dtype)


def interp_t(taps, weights, start, rows, mixed=False):
    row_ids = lax.broadcasted_iota(jnp.int32, (rows, ANGLES), 0)
    if mixed:
        ids = row_ids % CLASS_MAIN * CLASSES + row_ids // CLASS_MAIN
        for place in range(TAIL_PAD):
            value = TAIL_IDS[place] if place < TAIL else -ANGLES
            ids = jnp.where(row_ids == MAIN + place, value, ids)
        row_ids = ids
    row_ids += start
    total = jnp.zeros((rows, ANGLES), jnp.float32)
    for s in range(taps.shape[0]):
        total += jnp.where(row_ids == taps[s : s + 1, :], weights[s : s + 1, :], 0.0)
    return total


def phase_rows(cos_ref, sin_ref, shift, first, count, sign):
    freqs = cos_ref.shape[1]
    ranges = (
        (lax.broadcasted_iota(jnp.int32, (1, freqs), 1) + freqs).astype(jnp.float32)
        * (2.0 * math.pi / freqs)
        * shift
    )
    def turns(start, step, count):
        ids = lax.broadcasted_iota(jnp.int32, (count, 1), 0) * step + start
        angle = ids.astype(jnp.float32) / (2.0 * ANGLES) * ranges
        return jnp.cos(angle), jnp.sin(angle)

    def times(left, right):
        return left[0] * right[0] - left[1] * right[1], left[0] * right[1] + left[1] * right[0]

    offset = (0.5 / (2.0 * ANGLES) - 0.5) * ranges
    offset = (jnp.cos(offset) * ROOT_HALF, jnp.sin(offset) * ROOT_HALF)
    coarse = times(turns(first, 64, 8), offset)
    middle, fine = turns(0, 8, 8), turns(0, 1, 8)
    for group in range(count // 8):
        if group % 8 == 0:
            a = group // 8
            row = times((coarse[0][a : a + 1], coarse[1][a : a + 1]), middle)
        b = group % 8
        cosine, sine = times((row[0][b : b + 1], row[1][b : b + 1]), fine)
        cos_ref[group * 8 : group * 8 + 8, :] = cosine
        sin_ref[group * 8 : group * 8 + 8, :] = sign * sine


def table_kernel(
    shifts, taps, weights, ranges,
    range_out, m0, m1, m2, m3, m4, c0, s0, c1, s1, c2, s2, c3, s3, c4, s4, turned,
):
    band_pos, grp_pos = lax.axis_index("band"), lax.axis_index("grp")
    h0, h1, h2 = band_pos & 1, band_pos >> 1 & 1, band_pos >> 2 & 1
    h3, h4 = grp_pos & 1, grp_pos >> 1 & 1
    count = ranges.shape[0]
    depth = ranges.shape[1]
    for k in range(count):
        range_out[k * depth : (k + 1) * depth, :] = ranges[band_pos ^ k]

    def fill(out, level, half, start, rows, first, count, row=0):
        turned[:ANGLES, :rows] = interp_t(taps[level, half], weights[level, half], start, rows).T
        out[row : row + count, :rows] = turned[pl.ds(first, count), :rows].astype(jnp.bfloat16)

    first_start = FIRST_STARTS[0]
    for combo in range(1, len(FIRST_STARTS)):
        first_start = jnp.where(h1 + 2 * h2 == combo, FIRST_STARTS[combo], first_start)
    wide1 = pl.multiple_of(h1 * HALF + h2 * WIDE_STEP, 16)
    rows = MAIN + TAIL_PAD
    turned[:ANGLES, :rows] = interp_t(taps[0, h0], weights[0, h0], first_start, rows, True).T
    window = turned[pl.ds(wide1, WIDE), :rows].astype(jnp.bfloat16)
    main, tail = window[:, :MAIN], window[:, MAIN:]
    for at, sign in ((0, 1), (WIDE, -1)):
        m0[at : at + WIDE, :MAIN] = main
        m0[at : at + WIDE, MAIN : 2 * MAIN] = sign * main
        m0[at : at + WIDE, 2 * MAIN : 2 * MAIN + TAIL_PAD] = tail
        m0[at : at + WIDE, 2 * MAIN + TAIL_PAD :] = sign * tail
    phase_rows(c0, s0, shifts[0], h0 * ANGLES + wide1, WIDE, 1.0)

    half2 = pl.multiple_of(h2 * HALF, HALF)
    fill(m1, 1, h1, h2 * WIDE_STEP, WIDE, half2, HALF)
    phase_rows(c1, s1, shifts[1], h1 * ANGLES + half2, HALF, 1.0)

    turned[:ANGLES, :] = interp_t(taps[2, h2], weights[2, h2], 0, HALF).T
    turned[ANGLES:, :] = jnp.zeros((turned.shape[0] - ANGLES, HALF), jnp.float32)
    for k in range(MATES):
        mate = grp_pos ^ k
        half, side = mate & 1, mate >> 1 & 1
        rows = turned[pl.ds(pl.multiple_of(half * HALF, HALF), SENT_STEP + SENT_PAD), :]
        window = jnp.where(side == 1, rows[SENT_STEP:], rows[:SENT_PAD])
        m2[k * SENT_PAD : (k + 1) * SENT_PAD, :] = window.astype(jnp.bfloat16)
        first = h2 * ANGLES + half * HALF + side * SENT_STEP
        phase_rows(c2.at[k], s2.at[k], shifts[2], first, SENT_PAD, 1.0)

    half4 = pl.multiple_of(h4 * HALF, HALF)
    turned[:ANGLES, :SENT_PAD] = interp_t(taps[3, h3], weights[3, h3], h4 * SENT_STEP, SENT_PAD).T
    window = turned[pl.ds(half4, HALF), :SENT_PAD].astype(jnp.bfloat16)
    nothing = jnp.zeros((HALF, REST), jnp.bfloat16)
    for part in (0, 1):
        m3[part, :, :BULK] = window[:, :BULK]
        tail = BULK + part * REST
        m3[part, :, tail : tail + REST] = window[:, BULK:SENT]
        tail = BULK + (1 - part) * REST
        m3[part, :, tail : tail + REST] = nothing
    sign3 = (1 - 2 * h3).astype(jnp.float32)
    phase_rows(c3, s3, shifts[3], h3 * ANGLES + half4, HALF, sign3)
    fill(m4, 4, h4, 0, HALF, 0, ANGLES)
    sign4 = (1 - 2 * h4).astype(jnp.float32)
    phase_rows(c4, s4, shifts[4], h4 * ANGLES, ANGLES, sign4)


def send_order(count):
    return [6, 7, 5, 2, 4, 3, 1, 0] if count == SUBS else list(range(count - 1, -1, -1))


def dot(left, right):
    return jnp.dot(left, right, preferred_element_type=jnp.float32)


def turned_pair(total, diff, cosine, sine):
    freqs = cosine.shape[1]
    real = cosine * total[:, :freqs] - sine * diff[:, freqs:]
    imag = cosine * total[:, freqs:] + sine * diff[:, :freqs]
    return real, imag


def turn(out, rows, total, diff, cosine, sine):
    freqs = cosine.shape[1]
    real, imag = turned_pair(total, diff, cosine, sine)
    out[rows, :freqs] = real.astype(out.dtype)
    out[rows, freqs:] = imag.astype(out.dtype)


def merge_sent(out, low, high, m3, cosine, sine):
    freqs = cosine.shape[1]
    sides = []
    for mixed in (low + high, low - high):
        tail = mixed[2 * BULK :]
        for part in (0, 1):
            rows = jnp.concatenate([mixed[part * BULK : (part + 1) * BULK], tail], axis=0)
            sides.append(dot(m3[part], rows))
    total_real, total_imag, diff_real, diff_imag = sides
    out[:, :freqs] = (cosine * total_real - sine * diff_imag).astype(out.dtype)
    out[:, freqs:] = (cosine * total_imag + sine * diff_real).astype(out.dtype)


def band_kernel(*refs, sources):
    order = send_order(sources)
    blocks = [refs[order.index(k)] for k in range(sources)]
    ranges, m0, m1, m2, c0, s0, c1, s1, c2, s2 = refs[sources : sources + 10]
    outs = refs[sources + 10 : sources + 10 + MATES]
    wide, sub0, sub1, sub2 = refs[sources + 10 + MATES :]
    depth = ranges.shape[0] // sources
    freqs = c0.shape[1]
    scale = 1.0 / math.sqrt(freqs)
    width = blocks[0].shape[1]
    pieces = blocks[0].shape[0] // FIRST
    tails = SUBS * MAIN
    blank = jnp.zeros((TAIL_PAD - TAIL, depth), wide.dtype)
    for k in range(sources):
        lanes = slice(k * depth, (k + 1) * depth)
        ends = blocks[k][pieces * MAIN :, :]
        for t in range(SUBS):
            piece, at = divmod(t * depth, width)
            wide[t * MAIN : (t + 1) * MAIN, lanes] = blocks[k][
                piece * MAIN : (piece + 1) * MAIN, at : at + depth
            ]
            end = ends[piece * TAIL : (piece + 1) * TAIL, at : at + depth]
            row = tails + t * TAIL_PAD
            wide[row : row + TAIL_PAD, lanes] = jnp.concatenate([end, blank], axis=0)
    sub0[...] = (dot(wide[...], ranges[...]) * scale).astype(sub0.dtype)
    for p in range(SUBS // 2):
        main = sub0[2 * p * MAIN : 2 * (p + 1) * MAIN, :]
        tail = sub0[tails + 2 * p * TAIL_PAD : tails + 2 * (p + 1) * TAIL_PAD, :]
        both = dot(m0[...], jnp.concatenate([main, tail], axis=0))
        turn(sub1, slice(p * WIDE, (p + 1) * WIDE), both[:WIDE], both[WIDE:], c0[...], s0[...])
    for p in range(SUBS // 4):
        low = sub1[2 * p * WIDE : (2 * p + 1) * WIDE, :]
        high = sub1[(2 * p + 1) * WIDE : (2 * p + 2) * WIDE, :]
        rows = slice(p * HALF, (p + 1) * HALF)
        turn(sub2, rows, dot(m1[...], low + high), dot(m1[...], low - high), c1[...], s1[...])
    low, high = sub2[:HALF, :], sub2[HALF:, :]
    total, diff = low + high, low - high
    total, diff = dot(m2[...], total), dot(m2[...], diff)
    for k in range(MATES):
        rows = slice(k * SENT_PAD, (k + 1) * SENT_PAD)
        real, imag = turned_pair(total[rows], diff[rows], c2[k], s2[k])
        outs[k][:BULK, :] = real[:BULK].astype(sub2.dtype)
        outs[k][BULK : 2 * BULK, :] = imag[:BULK].astype(sub2.dtype)
        ends = jnp.concatenate([real[BULK:SENT], imag[BULK:SENT]], axis=0)
        outs[k][2 * BULK :, :] = ends.astype(sub2.dtype)


def own_kernel(along, own, m3, m4, c3, s3, part, sub4):
    merge_sent(sub4, own[...], along[...], m3, c3[...], s3[...])
    part[...] = dot(m4[...], sub4[...])


def grp_kernel(across, both, part, m3, m4, c3, s3, c4, s4, out_far, sub4, out, sems):
    freqs = c3.shape[1]
    merge_sent(sub4, across[...], both[...], m3, c3[...], s3[...])
    pieces = sems.shape[0]
    count = out.shape[1] // pieces
    copies = []
    for piece in range(pieces):
        rows = slice(piece * count, (piece + 1) * count)
        low = part[rows, :]
        high = dot(m4[rows, :], sub4[...])
        total, diff = low + high, low - high
        cosine, sine = c4[rows, :], s4[rows, :]
        out[0, rows, :] = (cosine * total[:, :freqs] - sine * diff[:, freqs:]).astype(out.dtype)
        out[1, rows, :] = (cosine * total[:, freqs:] + sine * diff[:, :freqs]).astype(out.dtype)
        copy = pltpu.make_async_copy(
            out.at[:, rows, :], out_far.at[:, rows, :], sems.at[piece]
        )
        copy.start()
        copies.append(copy)
    for copy in copies:
        copy.wait()


VMEM = pl.BlockSpec(memory_space=pltpu.VMEM)
FAR = pl.BlockSpec(memory_space=pltpu.HBM)
SMEM = pl.BlockSpec(memory_space=pltpu.SMEM)
PARAMS = pltpu.CompilerParams(vmem_limit_bytes=48 * 1024 * 1024)
BEAM_PARAMS = pltpu.CompilerParams(vmem_limit_bytes=55687168)


def swapped(block, axis, mask):
    count = lax.axis_size(axis)
    return lax.ppermute(block, axis, [(low, low ^ mask) for low in range(count)])


def on_device(raw, taps, weights, shifts):
    n_band = lax.axis_size("band")
    freqs = raw.shape[1]
    freq_count = freqs * n_band
    pulses = raw.shape[2] // n_band
    bf16, f32 = jnp.bfloat16, jnp.float32
    shape = jax.ShapeDtypeStruct
    lanes = SUBS * 2 * freqs
    pieces = max(1, lanes // 128)

    table = jnp.asarray(beam_rows(pulses))
    beams = pl.pallas_call(
        functools.partial(beam_kernel, pulses=pulses),
        out_shape=[shape((FIRST * pieces, lanes // pieces), bf16)] * n_band,
        in_specs=[FAR, FAR],
        out_specs=[VMEM] * n_band,
        scratch_shapes=[
            pltpu.VMEM(raw.shape, bf16),
            pltpu.VMEM(table.shape, bf16),
            pltpu.VMEM((CLASSES, lanes, 2 * pulses // CLASSES), bf16),
            pltpu.VMEM((CLASSES, SUBS * CLASS_PAD, lanes), f32),
            pltpu.SemaphoreType.DMA,
            pltpu.SemaphoreType.DMA,
        ],
        compiler_params=BEAM_PARAMS,
        cost_estimate=pl.CostEstimate(
            flops=SUBS * FIRST * pulses * lanes, bytes_accessed=1 << 21, transcendentals=0
        ),
        name="beam",
    )(raw, table)

    wide2 = 2 * freq_count
    tables = pl.pallas_call(
        table_kernel,
        out_shape=[
            shape((wide2, wide2), bf16),
            shape((2 * WIDE, 2 * (MAIN + TAIL_PAD)), bf16),
            shape((HALF, WIDE), bf16),
            shape((MATES * SENT_PAD, HALF), bf16),
            shape((2, HALF, SENT_PAD), bf16),
            shape((ANGLES, HALF), bf16),
        ]
        + [
            shape(rows + (freq_count,), f32)
            for rows in ((WIDE,), (HALF,), (MATES, SENT_PAD), (HALF,), (ANGLES,))
            for _ in range(2)
        ],
        in_specs=[SMEM, VMEM, VMEM, VMEM],
        out_specs=[VMEM] * 16,
        scratch_shapes=[pltpu.VMEM((ANGLES + 2 * REST, HALF), f32)],
        compiler_params=PARAMS,
        cost_estimate=pl.CostEstimate(
            flops=1 << 24, bytes_accessed=1 << 23, transcendentals=1 << 18
        ),
        name="tables",
    )(shifts, taps, weights, jnp.asarray(range_rows(freq_count, freqs)))
    ranges, m0, m1, m2, m3, m4, c0, s0, c1, s1, c2, s2, c3, s3, c4, s4 = tables

    blocks = [swapped(beams[k], "band", k) if k else beams[k] for k in send_order(n_band)]
    pieces = pl.pallas_call(
        functools.partial(band_kernel, sources=n_band),
        out_shape=[shape((2 * SENT, freq_count), bf16)] * MATES,
        in_specs=[VMEM] * (n_band + 10),
        out_specs=[VMEM] * MATES,
        scratch_shapes=[
            pltpu.VMEM((SUBS * (MAIN + TAIL_PAD), wide2), bf16),
            pltpu.VMEM((SUBS * (MAIN + TAIL_PAD), wide2), bf16),
            pltpu.VMEM((SUBS // 2 * WIDE, wide2), bf16),
            pltpu.VMEM((SUBS // 4 * HALF, wide2), bf16),
        ],
        compiler_params=PARAMS,
        cost_estimate=pl.CostEstimate(flops=1 << 31, bytes_accessed=1 << 22, transcendentals=0),
        name="band_merges",
    )(*blocks, ranges, m0, m1, m2, c0, s0, c1, s1, c2, s2)

    halves = [swapped(pieces[k], "grp", k) for k in range(1, MATES)] + [pieces[0]]
    along, across, both, own = halves
    part = pl.pallas_call(
        own_kernel,
        out_shape=shape((ANGLES, wide2), f32),
        in_specs=[VMEM] * 6,
        out_specs=VMEM,
        scratch_shapes=[pltpu.VMEM((HALF, wide2), bf16)],
        compiler_params=PARAMS,
        cost_estimate=pl.CostEstimate(flops=1 << 29, bytes_accessed=1 << 21, transcendentals=0),
        name="own_merge",
    )(along, own, m3, m4, c3, s3)
    return pl.pallas_call(
        grp_kernel,
        out_shape=shape((2, ANGLES, freq_count), bf16),
        in_specs=[VMEM] * 9,
        out_specs=FAR,
        scratch_shapes=[
            pltpu.VMEM((HALF, wide2), bf16),
            pltpu.VMEM((2, ANGLES, freq_count), bf16),
            pltpu.SemaphoreType.DMA((4,)),
        ],
        compiler_params=PARAMS,
        cost_estimate=pl.CostEstimate(flops=1 << 29, bytes_accessed=1 << 21, transcendentals=0),
        name="grp_merges",
    )(across, both, part, m3, m4, c3, s3, c4, s4)


def solution(mesh):
    in_specs = (P(None, "band", "grp"), P(), P(), P())
    out_specs = P(None, ("grp", "band"), None)
    return jax.shard_map(
        on_device, mesh=mesh, in_specs=in_specs, out_specs=out_specs, check_vma=False
    )
```

```python
import functools
import math

import jax
import jax.numpy as jnp
import ml_dtypes
import numpy as np
from jax import lax
from jax.experimental import pallas as pl
from jax.experimental.pallas import tpu as pltpu
from jax.sharding import PartitionSpec as P

ANGLES = 512
HALF = ANGLES // 2
BAND_LEVELS = 3
GRP_LEVELS = 2
LEVELS = BAND_LEVELS + GRP_LEVELS
SUBS = 1 << BAND_LEVELS
MATES = 1 << GRP_LEVELS
ROOT_HALF = 0.7071067811865476


def up_to(value, unit):
    return -(-value // unit) * unit


def rows_read(low, high):
    return max(0, low // 2 - 1), min(HALF - 1, (high + 1) // 2 + 2)


WIDE = up_to(rows_read(0, HALF - 1)[1] + 1, 16)
WIDE_STEP = HALF - WIDE
SENT = up_to(rows_read(0, HALF - 1)[1] + 1, 8)
SENT_STEP = HALF - SENT
BULK = SENT // 16 * 16
REST = SENT - BULK
SENT_PAD = BULK + 2 * REST


def first_windows():
    spans = []
    for h2 in (0, 1):
        low, high = rows_read(h2 * HALF, h2 * HALF + HALF - 1)
        for h1 in (0, 1):
            spans.append(rows_read(h1 * HALF + low, h1 * HALF + high))
    rows = up_to(max(high - low + 1 + low % 2 for low, high in spans), 8)
    return [min(low - low % 2, HALF - rows) for low, high in spans], rows


FIRST_STARTS, FIRST = first_windows()
CLASSES = 4
CLASS_MAIN = FIRST // (16 * CLASSES) * 16
MAIN = CLASSES * CLASS_MAIN
CLASS_ROWS = [len(range(u, FIRST, CLASSES)) for u in range(CLASSES)]
CLASS_PAD = up_to(max(CLASS_ROWS), 8)
TAIL_IDS = [CLASSES * m + u for u in range(CLASSES) for m in range(CLASS_MAIN, CLASS_ROWS[u])]
TAIL = len(TAIL_IDS)
TAIL_PAD = up_to(TAIL, 16)


def beam_rows(pulses):
    pulse_ids = np.arange(pulses // CLASSES)
    table = np.zeros((CLASSES, SUBS, CLASS_PAD, 2 * len(pulse_ids)))
    for sector in range(SUBS):
        start = (sector & 1) * HALF + FIRST_STARTS[sector >> 1]
        for u in range(CLASSES):
            angle_ids = start + u + CLASSES * np.arange(CLASS_ROWS[u])
            phases = (angle_ids[:, None] * pulse_ids[None, :] % ANGLES) * (2.0 * math.pi / ANGLES)
            rows = np.concatenate([np.cos(phases), np.sin(phases)], axis=1)
            table[(start + u) % CLASSES, sector, : len(rows)] = rows
    return table.reshape(CLASSES, SUBS * CLASS_PAD, -1).astype(ml_dtypes.bfloat16)


def range_rows(freq_count, freq_local):
    ids = np.arange(freq_count)
    phases = (ids[:, None] * ids[None, :] % freq_count) * (2.0 * math.pi / freq_count)
    cosine, sine = np.cos(phases), np.sin(phases)
    table = np.stack(
        [np.concatenate([cosine, -sine], axis=1), np.concatenate([sine, cosine], axis=1)]
    )
    table = table.reshape(2, freq_count // freq_local, freq_local, 2 * freq_count)
    table = table.transpose(1, 0, 2, 3).reshape(-1, 2 * freq_local, 2 * freq_count)
    return table.astype(ml_dtypes.bfloat16)


def beam_kernel(raw_far, table_far, *refs, pulses):
    outs, (raw, table, rhs, acc, raw_sem, table_sem) = refs[:-6], refs[-6:]
    freqs = raw.shape[1]
    quarter = pulses // CLASSES
    band_pos = lax.axis_index("band")
    scale = 1.0 / math.sqrt(pulses)
    raw_copy = pltpu.make_async_copy(raw_far, raw, raw_sem)
    raw_copy.start()
    table_copy = pltpu.make_async_copy(table_far, table, table_sem)
    table_copy.start()
    raw_copy.wait()
    for upper in range(len(outs) // SUBS):
        block = band_pos // SUBS ^ upper if len(outs) > SUBS else 0
        for t in range(SUBS):
            at = pl.multiple_of((block * SUBS + t) * pulses, pulses)
            row = t * 2 * freqs
            x0, x1, x2, x3 = (
                raw[:, :, pl.ds(at + j * quarter, quarter)].astype(jnp.float32)
                for j in range(CLASSES)
            )
            even, odd, even_diff, odd_diff = x0 + x2, x1 + x3, x0 - x2, x1 - x3
            for u, (real, imag) in enumerate(
                (
                    (even[0] + odd[0], even[1] + odd[1]),
                    (even_diff[0] + odd_diff[1], even_diff[1] - odd_diff[0]),
                    (even[0] - odd[0], even[1] - odd[1]),
                    (even_diff[0] - odd_diff[1], even_diff[1] + odd_diff[0]),
                )
            ):
                real, imag = real.astype(rhs.dtype), imag.astype(rhs.dtype)
                rhs[u, row : row + freqs, :quarter] = real
                rhs[u, row : row + freqs, quarter:] = imag
                rhs[u, row + freqs : row + 2 * freqs, :quarter] = imag
                rhs[u, row + freqs : row + 2 * freqs, quarter:] = -real
        if upper == 0:
            table_copy.wait()
        for u in range(CLASSES):
            acc[u] = lax.dot_general(
                table[u],
                rhs[u],
                (((1,), (1,)), ((), ())),
                preferred_element_type=jnp.float32,
            )
        for low in range(SUBS):
            sector = (band_pos ^ low) & (SUBS - 1)
            rows = pl.ds(pl.multiple_of(sector * CLASS_PAD, 8), CLASS_PAD)
            shift = FIRST_STARTS[0] % CLASSES
            for combo in range(1, len(FIRST_STARTS)):
                shift = jnp.where(sector >> 1 == combo, FIRST_STARTS[combo] % CLASSES, shift)
            classes = [
                acc[(shift + u) & (CLASSES - 1), rows, :] * scale for u in range(CLASSES)
            ]
            out = outs[upper * SUBS + low]
            width = out.shape[1]
            pieces = acc.shape[2] // width
            tails = []
            for piece in range(pieces):
                lanes = slice(piece * width, (piece + 1) * width)
                for u, values in enumerate(classes):
                    at = piece * MAIN + u * CLASS_MAIN
                    out[at : at + CLASS_MAIN, :] = values[:CLASS_MAIN, lanes].astype(out.dtype)
                    tails.append(values[CLASS_MAIN : CLASS_ROWS[u], lanes])
            out[pieces * MAIN :, :] = jnp.concatenate(tails, axis=0).astype(out.dtype)


def interp_t(taps, weights, start, rows, mixed=False):
    row_ids = lax.broadcasted_iota(jnp.int32, (rows, ANGLES), 0)
    if mixed:
        ids = row_ids % CLASS_MAIN * CLASSES + row_ids // CLASS_MAIN
        for place in range(TAIL_PAD):
            value = TAIL_IDS[place] if place < TAIL else -ANGLES
            ids = jnp.where(row_ids == MAIN + place, value, ids)
        row_ids = ids
    row_ids += start
    total = jnp.zeros((rows, ANGLES), jnp.float32)
    for s in range(taps.shape[0]):
        total += jnp.where(row_ids == taps[s : s + 1, :], weights[s : s + 1, :], 0.0)
    return total


def phase_rows(cos_ref, sin_ref, shift, first, count, sign):
    freqs = cos_ref.shape[1]
    ranges = (
        (lax.broadcasted_iota(jnp.int32, (1, freqs), 1) + freqs).astype(jnp.float32)
        * (2.0 * math.pi / freqs)
        * shift
    )
    def turns(start, step, count):
        ids = lax.broadcasted_iota(jnp.int32, (count, 1), 0) * step + start
        angle = ids.astype(jnp.float32) / (2.0 * ANGLES) * ranges
        return jnp.cos(angle), jnp.sin(angle)

    def times(left, right):
        return left[0] * right[0] - left[1] * right[1], left[0] * right[1] + left[1] * right[0]

    offset = (0.5 / (2.0 * ANGLES) - 0.5) * ranges
    offset = (jnp.cos(offset) * ROOT_HALF, jnp.sin(offset) * ROOT_HALF)
    coarse = times(turns(first, 64, 8), offset)
    middle, fine = turns(0, 8, 8), turns(0, 1, 8)
    for group in range(count // 8):
        if group % 8 == 0:
            a = group // 8
            row = times((coarse[0][a : a + 1], coarse[1][a : a + 1]), middle)
        b = group % 8
        cosine, sine = times((row[0][b : b + 1], row[1][b : b + 1]), fine)
        cos_ref[group * 8 : group * 8 + 8, :] = cosine
        sin_ref[group * 8 : group * 8 + 8, :] = sign * sine


def table_kernel(
    shifts, taps, weights, ranges,
    range_out, m0, m1, m2, m3, m4, c0, s0, c1, s1, c2, s2, c3, s3, c4, s4, turned,
):
    band_pos, grp_pos = lax.axis_index("band"), lax.axis_index("grp")
    h0, h1, h2 = band_pos & 1, band_pos >> 1 & 1, band_pos >> 2 & 1
    h3, h4 = grp_pos & 1, grp_pos >> 1 & 1
    count = ranges.shape[0]
    depth = ranges.shape[1]
    for k in range(count):
        range_out[k * depth : (k + 1) * depth, :] = ranges[band_pos ^ k]

    def fill(out, level, half, start, rows, first, count, row=0):
        turned[:ANGLES, :rows] = interp_t(taps[level, half], weights[level, half], start, rows).T
        out[row : row + count, :rows] = turned[pl.ds(first, count), :rows].astype(jnp.bfloat16)

    first_start = FIRST_STARTS[0]
    for combo in range(1, len(FIRST_STARTS)):
        first_start = jnp.where(h1 + 2 * h2 == combo, FIRST_STARTS[combo], first_start)
    wide1 = pl.multiple_of(h1 * HALF + h2 * WIDE_STEP, 16)
    rows = MAIN + TAIL_PAD
    turned[:ANGLES, :rows] = interp_t(taps[0, h0], weights[0, h0], first_start, rows, True).T
    window = turned[pl.ds(wide1, WIDE), :rows].astype(jnp.bfloat16)
    main, tail = window[:, :MAIN], window[:, MAIN:]
    for at, sign in ((0, 1), (WIDE, -1)):
        m0[at : at + WIDE, :MAIN] = main
        m0[at : at + WIDE, MAIN : 2 * MAIN] = sign * main
        m0[at : at + WIDE, 2 * MAIN : 2 * MAIN + TAIL_PAD] = tail
        m0[at : at + WIDE, 2 * MAIN + TAIL_PAD :] = sign * tail
    phase_rows(c0, s0, shifts[0], h0 * ANGLES + wide1, WIDE, 1.0)

    half2 = pl.multiple_of(h2 * HALF, HALF)
    fill(m1, 1, h1, h2 * WIDE_STEP, WIDE, half2, HALF)
    phase_rows(c1, s1, shifts[1], h1 * ANGLES + half2, HALF, 1.0)

    turned[:ANGLES, :] = interp_t(taps[2, h2], weights[2, h2], 0, HALF).T
    turned[ANGLES:, :] = jnp.zeros((turned.shape[0] - ANGLES, HALF), jnp.float32)
    for k in range(MATES):
        mate = grp_pos ^ k
        half, side = mate & 1, mate >> 1 & 1
        rows = turned[pl.ds(pl.multiple_of(half * HALF, HALF), SENT_STEP + SENT_PAD), :]
        window = jnp.where(side == 1, rows[SENT_STEP:], rows[:SENT_PAD])
        m2[k * SENT_PAD : (k + 1) * SENT_PAD, :] = window.astype(jnp.bfloat16)
        first = h2 * ANGLES + half * HALF + side * SENT_STEP
        phase_rows(c2.at[k], s2.at[k], shifts[2], first, SENT_PAD, 1.0)

    half4 = pl.multiple_of(h4 * HALF, HALF)
    turned[:ANGLES, :SENT_PAD] = interp_t(taps[3, h3], weights[3, h3], h4 * SENT_STEP, SENT_PAD).T
    window = turned[pl.ds(half4, HALF), :SENT_PAD].astype(jnp.bfloat16)
    nothing = jnp.zeros((HALF, REST), jnp.bfloat16)
    for part in (0, 1):
        m3[part, :, :BULK] = window[:, :BULK]
        tail = BULK + part * REST
        m3[part, :, tail : tail + REST] = window[:, BULK:SENT]
        tail = BULK + (1 - part) * REST
        m3[part, :, tail : tail + REST] = nothing
    sign3 = (1 - 2 * h3).astype(jnp.float32)
    phase_rows(c3, s3, shifts[3], h3 * ANGLES + half4, HALF, sign3)
    fill(m4, 4, h4, 0, HALF, 0, ANGLES)
    sign4 = (1 - 2 * h4).astype(jnp.float32)
    phase_rows(c4, s4, shifts[4], h4 * ANGLES, ANGLES, sign4)


def send_order(count):
    return [6, 7, 5, 3, 4, 2, 1, 0] if count == SUBS else list(range(count - 1, -1, -1))


def dot(left, right):
    return jnp.dot(left, right, preferred_element_type=jnp.float32)


def turned_pair(total, diff, cosine, sine):
    freqs = cosine.shape[1]
    real = cosine * total[:, :freqs] - sine * diff[:, freqs:]
    imag = cosine * total[:, freqs:] + sine * diff[:, :freqs]
    return real, imag


def turn(out, rows, total, diff, cosine, sine):
    freqs = cosine.shape[1]
    real, imag = turned_pair(total, diff, cosine, sine)
    out[rows, :freqs] = real.astype(out.dtype)
    out[rows, freqs:] = imag.astype(out.dtype)


def merge_sent(out, low, high, m3, cosine, sine):
    freqs = cosine.shape[1]
    sides = []
    for mixed in (low + high, low - high):
        tail = mixed[2 * BULK :]
        for part in (0, 1):
            rows = jnp.concatenate([mixed[part * BULK : (part + 1) * BULK], tail], axis=0)
            sides.append(dot(m3[part], rows))
    total_real, total_imag, diff_real, diff_imag = sides
    out[:, :freqs] = (cosine * total_real - sine * diff_imag).astype(out.dtype)
    out[:, freqs:] = (cosine * total_imag + sine * diff_real).astype(out.dtype)


def band_kernel(*refs, sources):
    order = send_order(sources)
    blocks = [refs[order.index(k)] for k in range(sources)]
    ranges, m0, m1, m2, c0, s0, c1, s1, c2, s2 = refs[sources : sources + 10]
    outs = refs[sources + 10 : sources + 10 + MATES]
    wide, sub0, sub1, sub2 = refs[sources + 10 + MATES :]
    depth = ranges.shape[0] // sources
    freqs = c0.shape[1]
    scale = 1.0 / math.sqrt(freqs)
    width = blocks[0].shape[1]
    pieces = blocks[0].shape[0] // FIRST
    tails = SUBS * MAIN
    blank = jnp.zeros((TAIL_PAD - TAIL, depth), wide.dtype)
    for k in range(sources):
        lanes = slice(k * depth, (k + 1) * depth)
        ends = blocks[k][pieces * MAIN :, :]
        for t in range(SUBS):
            piece, at = divmod(t * depth, width)
            wide[t * MAIN : (t + 1) * MAIN, lanes] = blocks[k][
                piece * MAIN : (piece + 1) * MAIN, at : at + depth
            ]
            end = ends[piece * TAIL : (piece + 1) * TAIL, at : at + depth]
            row = tails + t * TAIL_PAD
            wide[row : row + TAIL_PAD, lanes] = jnp.concatenate([end, blank], axis=0)
    sub0[...] = (dot(wide[...], ranges[...]) * scale).astype(sub0.dtype)
    for p in range(SUBS // 2):
        main = sub0[2 * p * MAIN : 2 * (p + 1) * MAIN, :]
        tail = sub0[tails + 2 * p * TAIL_PAD : tails + 2 * (p + 1) * TAIL_PAD, :]
        both = dot(m0[...], jnp.concatenate([main, tail], axis=0))
        turn(sub1, slice(p * WIDE, (p + 1) * WIDE), both[:WIDE], both[WIDE:], c0[...], s0[...])
    for p in range(SUBS // 4):
        low = sub1[2 * p * WIDE : (2 * p + 1) * WIDE, :]
        high = sub1[(2 * p + 1) * WIDE : (2 * p + 2) * WIDE, :]
        rows = slice(p * HALF, (p + 1) * HALF)
        turn(sub2, rows, dot(m1[...], low + high), dot(m1[...], low - high), c1[...], s1[...])
    low, high = sub2[:HALF, :], sub2[HALF:, :]
    total, diff = low + high, low - high
    total, diff = dot(m2[...], total), dot(m2[...], diff)
    for k in range(MATES):
        rows = slice(k * SENT_PAD, (k + 1) * SENT_PAD)
        real, imag = turned_pair(total[rows], diff[rows], c2[k], s2[k])
        outs[k][:BULK, :] = real[:BULK].astype(sub2.dtype)
        outs[k][BULK : 2 * BULK, :] = imag[:BULK].astype(sub2.dtype)
        ends = jnp.concatenate([real[BULK:SENT], imag[BULK:SENT]], axis=0)
        outs[k][2 * BULK :, :] = ends.astype(sub2.dtype)


def own_kernel(along, own, m3, m4, c3, s3, part, sub4):
    merge_sent(sub4, own[...], along[...], m3, c3[...], s3[...])
    part[...] = dot(m4[...], sub4[...])


def grp_kernel(across, both, part, m3, m4, c3, s3, c4, s4, out_far, sub4, out, sems):
    freqs = c3.shape[1]
    merge_sent(sub4, across[...], both[...], m3, c3[...], s3[...])
    pieces = sems.shape[0]
    count = out.shape[1] // pieces
    copies = []
    for piece in range(pieces):
        rows = slice(piece * count, (piece + 1) * count)
        low = part[rows, :]
        high = dot(m4[rows, :], sub4[...])
        total, diff = low + high, low - high
        cosine, sine = c4[rows, :], s4[rows, :]
        out[0, rows, :] = (cosine * total[:, :freqs] - sine * diff[:, freqs:]).astype(out.dtype)
        out[1, rows, :] = (cosine * total[:, freqs:] + sine * diff[:, :freqs]).astype(out.dtype)
        copy = pltpu.make_async_copy(
            out.at[:, rows, :], out_far.at[:, rows, :], sems.at[piece]
        )
        copy.start()
        copies.append(copy)
    for copy in copies:
        copy.wait()


VMEM = pl.BlockSpec(memory_space=pltpu.VMEM)
FAR = pl.BlockSpec(memory_space=pltpu.HBM)
SMEM = pl.BlockSpec(memory_space=pltpu.SMEM)
PARAMS = pltpu.CompilerParams(vmem_limit_bytes=48 * 1024 * 1024)
BEAM_PARAMS = pltpu.CompilerParams(vmem_limit_bytes=55687168)


def swapped(block, axis, mask):
    count = lax.axis_size(axis)
    return lax.ppermute(block, axis, [(low, low ^ mask) for low in range(count)])


def on_device(raw, taps, weights, shifts):
    n_band = lax.axis_size("band")
    freqs = raw.shape[1]
    freq_count = freqs * n_band
    pulses = raw.shape[2] // n_band
    bf16, f32 = jnp.bfloat16, jnp.float32
    shape = jax.ShapeDtypeStruct
    lanes = SUBS * 2 * freqs
    pieces = max(1, lanes // 128)

    table = jnp.asarray(beam_rows(pulses))
    beams = pl.pallas_call(
        functools.partial(beam_kernel, pulses=pulses),
        out_shape=[shape((FIRST * pieces, lanes // pieces), bf16)] * n_band,
        in_specs=[FAR, FAR],
        out_specs=[VMEM] * n_band,
        scratch_shapes=[
            pltpu.VMEM(raw.shape, bf16),
            pltpu.VMEM(table.shape, bf16),
            pltpu.VMEM((CLASSES, lanes, 2 * pulses // CLASSES), bf16),
            pltpu.VMEM((CLASSES, SUBS * CLASS_PAD, lanes), f32),
            pltpu.SemaphoreType.DMA,
            pltpu.SemaphoreType.DMA,
        ],
        compiler_params=BEAM_PARAMS,
        cost_estimate=pl.CostEstimate(
            flops=SUBS * FIRST * pulses * lanes, bytes_accessed=1 << 21, transcendentals=0
        ),
        name="beam",
    )(raw, table)

    wide2 = 2 * freq_count
    tables = pl.pallas_call(
        table_kernel,
        out_shape=[
            shape((wide2, wide2), bf16),
            shape((2 * WIDE, 2 * (MAIN + TAIL_PAD)), bf16),
            shape((HALF, WIDE), bf16),
            shape((MATES * SENT_PAD, HALF), bf16),
            shape((2, HALF, SENT_PAD), bf16),
            shape((ANGLES, HALF), bf16),
        ]
        + [
            shape(rows + (freq_count,), f32)
            for rows in ((WIDE,), (HALF,), (MATES, SENT_PAD), (HALF,), (ANGLES,))
            for _ in range(2)
        ],
        in_specs=[SMEM, VMEM, VMEM, VMEM],
        out_specs=[VMEM] * 16,
        scratch_shapes=[pltpu.VMEM((ANGLES + 2 * REST, HALF), f32)],
        compiler_params=PARAMS,
        cost_estimate=pl.CostEstimate(
            flops=1 << 24, bytes_accessed=1 << 23, transcendentals=1 << 18
        ),
        name="tables",
    )(shifts, taps, weights, jnp.asarray(range_rows(freq_count, freqs)))
    ranges, m0, m1, m2, m3, m4, c0, s0, c1, s1, c2, s2, c3, s3, c4, s4 = tables

    blocks = [swapped(beams[k], "band", k) if k else beams[k] for k in send_order(n_band)]
    pieces = pl.pallas_call(
        functools.partial(band_kernel, sources=n_band),
        out_shape=[shape((2 * SENT, freq_count), bf16)] * MATES,
        in_specs=[VMEM] * (n_band + 10),
        out_specs=[VMEM] * MATES,
        scratch_shapes=[
            pltpu.VMEM((SUBS * (MAIN + TAIL_PAD), wide2), bf16),
            pltpu.VMEM((SUBS * (MAIN + TAIL_PAD), wide2), bf16),
            pltpu.VMEM((SUBS // 2 * WIDE, wide2), bf16),
            pltpu.VMEM((SUBS // 4 * HALF, wide2), bf16),
        ],
        compiler_params=PARAMS,
        cost_estimate=pl.CostEstimate(flops=1 << 31, bytes_accessed=1 << 22, transcendentals=0),
        name="band_merges",
    )(*blocks, ranges, m0, m1, m2, c0, s0, c1, s1, c2, s2)

    halves = [swapped(pieces[k], "grp", k) for k in range(1, MATES)] + [pieces[0]]
    along, across, both, own = halves
    part = pl.pallas_call(
        own_kernel,
        out_shape=shape((ANGLES, wide2), f32),
        in_specs=[VMEM] * 6,
        out_specs=VMEM,
        scratch_shapes=[pltpu.VMEM((HALF, wide2), bf16)],
        compiler_params=PARAMS,
        cost_estimate=pl.CostEstimate(flops=1 << 29, bytes_accessed=1 << 21, transcendentals=0),
        name="own_merge",
    )(along, own, m3, m4, c3, s3)
    return pl.pallas_call(
        grp_kernel,
        out_shape=shape((2, ANGLES, freq_count), bf16),
        in_specs=[VMEM] * 9,
        out_specs=FAR,
        scratch_shapes=[
            pltpu.VMEM((HALF, wide2), bf16),
            pltpu.VMEM((2, ANGLES, freq_count), bf16),
            pltpu.SemaphoreType.DMA((2,)),
        ],
        compiler_params=PARAMS,
        cost_estimate=pl.CostEstimate(flops=1 << 29, bytes_accessed=1 << 21, transcendentals=0),
        name="grp_merges",
    )(across, both, part, m3, m4, c3, s3, c4, s4)


def solution(mesh):
    in_specs = (P(None, "band", "grp"), P(), P(), P())
    out_specs = P(None, ("grp", "band"), None)
    return jax.shard_map(
        on_device, mesh=mesh, in_specs=in_specs, out_specs=out_specs, check_vma=False
    )
```
